512 devices in a mesh: panel: 64 (over z, x, core), sample: 8 (over y).
Axes of the slice: x: 4, y: 8, z: 8, core: 2. Of those that a mesh axis runs over, the one named last changes fastest.
Arguments:
- leaf_rhs: float32 [128, 256, 1024], P('panel', None, 'sample'), may hold values from -6 to 6
- sep_rhs: float32 [64, 256, 1024], P('panel', None, 'sample'), may hold values from -6 to 6
- leaf_size: int32 [128], P('panel'), may hold values from 64 to 256, as said below
- leaf_lower_inv: bfloat16 [128, 256, 256], P('panel'), may hold values from -0.375 to 0.375
- leaf_lower: bfloat16 [128, 2, 256, 256], P('panel'), may hold values from -0.1875 to 0.1875
- leaf_upper: bfloat16 [128, 2, 256, 256], P('panel'), may hold values from -0.25 to 0.25
- leaf_upper_inv: bfloat16 [128, 256, 256], P('panel'), may hold values from -0.375 to 0.375
- sep_lower_inv: float32 [64, 256, 256], P('panel', 'sample')
- sep_lower: float32 [64, 256, 256], P('panel', 'sample')
- sep_upper_inv: float32 [64, 256, 256], P('panel', 'sample')
- sep_upper: float32 [64, 256, 256], P('panel', 'sample')
Outputs:
- leaf_correction: float32 [128, 256, 1024], P('panel', None, 'sample')
- sep_correction: float32 [64, 256, 1024], P('panel', None, 'sample')
The draws below stay inside these ranges and needn't reach their ends.
Inputs may be any that keep to these rules, and one draw needn't show every extreme that they name: `leaf_size`: every subdomain holds a leaf with all 256 columns live.
All inputs are finite; a program needn't handle non-finite values.
Results may differ from the reference program's by a relative error of at most 0.0049.
Values may be sent and summed in bfloat16 or wider, within the bound.
No kernel may reach another device: no remote copies, remote signals or barrier semaphores. Data moves between devices by JAX's collectives and lax.ppermute only.
A program may use at most 128 MiB of HBM per device.

```python
import math
import jax
import jax.numpy as jnp
from jax import lax

W = 256
LEAF_DEV = 2
SEPS = 64
NLEAF = 128
SAMPLES = 1024


def chain_rates(key, tag, share):
    key = jax.random.fold_in(key, tag)
    first, second, third, fourth = jax.random.split(key, 4)
    scaling = jax.random.uniform(first, (SEPS, W), jnp.float32, 0.3, 0.6)
    slowness = jax.random.uniform(second, (SEPS, W), jnp.float32) < share
    reach = jnp.exp(math.log(0.25) / SEPS * jax.random.uniform(third, (SEPS, W), jnp.float32, 0.5, 1.5))
    quick = jax.random.uniform(fourth, (SEPS, W), jnp.float32, 0.2, 0.5)
    return (scaling, jnp.where(slowness, reach, quick))


def diagonal_block(key, diagonal, spread):
    noise = jax.random.normal(key, (SEPS, W, W), jnp.float32) * (0.03 / math.sqrt(W))
    identity = jnp.eye(W, dtype=jnp.float32)[None]
    return diagonal[:, :, None] * identity + noise * spread[:, :, None]


def draw_leaf_size(key, part):
    key = jax.random.fold_in(key, 5)
    first, second = jax.random.split(key)
    sizes = jax.random.randint(first, (SEPS, LEAF_DEV), W // 4, W + 1)
    fullest = jax.random.randint(second, (SEPS,), 0, LEAF_DEV)
    sizes = jnp.where(jnp.arange(LEAF_DEV)[None, :] == fullest[:, None], W, sizes)
    return sizes.reshape(-1).astype(jnp.int32)


def draw_sep_lower_inv(key, part):
    share = 0.5
    scaling, keeping = chain_rates(key, 11, share)
    key = jax.random.fold_in(key, 1)
    return diagonal_block(key, scaling, scaling)


def draw_sep_lower(key, part):
    share = 0.5
    scaling, keeping = chain_rates(key, 11, share)
    key = jax.random.fold_in(key, 2)
    return diagonal_block(key, -keeping / scaling, 1.0 / scaling)


def draw_sep_upper_inv(key, part):
    share = 0.5
    scaling, keeping = chain_rates(key, 12, share)
    key = jax.random.fold_in(key, 3)
    return diagonal_block(key, scaling, scaling)


def draw_sep_upper(key, part):
    share = 0.5
    scaling, keeping = chain_rates(key, 12, share)
    key = jax.random.fold_in(key, 4)
    return diagonal_block(key, -keeping / scaling, 1.0 / scaling)


def shard_levels(key, extent, cuts, smallest, top_value):
    loudness, own = 1.0, jax.random.fold_in(key, 6)
    for dim, blocks in cuts:
        draws = jnp.exp(jax.random.uniform(jax.random.fold_in(own, dim), (blocks,), jnp.float32, smallest / len(cuts), top_value / len(cuts)))
        loudness = loudness * jnp.repeat(draws, extent[dim] // blocks).reshape([-1 if axis == dim else 1 for axis in range(len(extent))])
    return loudness


def gaussian(key, dims, scale, most, cuts=(), kind=jnp.bfloat16):
    entries = scale * jax.random.normal(key, dims, jnp.float32)
    if cuts:
        entries = entries * shard_levels(key, dims, cuts, -0.22, 0.18)
    return jnp.clip(entries, -most, most).astype(kind)


def setup_inputs(seed: int = 0) -> dict:
    key_list = jax.random.split(jax.random.key(seed), 12)
    return {
        "leaf_rhs": gaussian(key_list[0], (NLEAF, W, SAMPLES), 1.0, 6.0, ((0, 64), (2, 8)), jnp.float32),
        "sep_rhs": gaussian(key_list[1], (SEPS, W, SAMPLES), 1.0, 6.0, ((0, 64), (2, 8)), jnp.float32),
        "leaf_size": draw_leaf_size(jax.random.fold_in(key_list[11], 71), 0),
        "leaf_lower_inv": gaussian(key_list[3], (NLEAF, W, W), W ** -0.5, 0.375, ((0, 64),)),
        "leaf_lower": gaussian(key_list[4], (NLEAF, 2, W, W), (2 * LEAF_DEV * W) ** -0.5, 0.1875, ((0, 64),)),
        "leaf_upper": gaussian(key_list[5], (NLEAF, 2, W, W), (2 * W) ** -0.5, 0.25, ((0, 64),)),
        "leaf_upper_inv": gaussian(key_list[6], (NLEAF, W, W), W ** -0.5, 0.375, ((0, 64),)),
        "sep_lower_inv": draw_sep_lower_inv(jax.random.fold_in(key_list[11], 71), 0),
        "sep_lower": draw_sep_lower(jax.random.fold_in(key_list[11], 71), 0),
        "sep_upper_inv": draw_sep_upper_inv(jax.random.fold_in(key_list[11], 71), 0),
        "sep_upper": draw_sep_upper(jax.random.fold_in(key_list[11], 71), 0),
    }


def exact(left_side, right_side):
    return jnp.dot(left_side, right_side, precision=lax.Precision.HIGHEST, preferred_element_type=jnp.float32)


def reference(leaf_rhs, sep_rhs, leaf_size, leaf_lower_inv, leaf_lower, leaf_upper, leaf_upper_inv, sep_lower_inv, sep_lower, sep_upper_inv, sep_upper):
    active_rows = (jnp.arange(W, dtype=jnp.int32)[None, :] < leaf_size[:, None]).astype(jnp.float32)[:, :, None]
    leaf_rounded = (active_rows * leaf_rhs).astype(jnp.bfloat16)
    leaf_forward = active_rows * jnp.einsum("lij,ljs->lis", leaf_lower_inv.astype(jnp.float32), leaf_rounded.astype(jnp.float32))
    forward_rounded = lax.optimization_barrier(leaf_forward.astype(jnp.bfloat16)).astype(jnp.float32)
    blocks = forward_rounded.reshape(SEPS, LEAF_DEV, W, SAMPLES)
    lower_blocks = leaf_lower.reshape(SEPS, LEAF_DEV, 2, W, W)
    own_terms = jnp.einsum("bmij,bmjs->bis", lower_blocks[:, :, 1].astype(jnp.float32), blocks)
    left_terms = jnp.einsum("bmij,bmjs->bis", lower_blocks[:, :, 0].astype(jnp.float32), blocks)
    left_next = jnp.concatenate([left_terms[1:], jnp.zeros((1, W, SAMPLES), jnp.float32)], axis=0)
    sep_source = sep_rhs - own_terms - left_next

    def forward_step(carried, pieces):
        inverse, coupling, source = pieces
        value = exact(inverse, source - exact(coupling, carried))
        return value, value

    _, sep_forward = lax.scan(forward_step, jnp.zeros((W, SAMPLES), jnp.float32), (sep_lower_inv, sep_lower, sep_source))

    def backward_step(carried, pieces):
        inverse, coupling, source = pieces
        value = exact(inverse, source - exact(coupling, carried))
        return value, value

    _, sep_correction = lax.scan(backward_step, jnp.zeros((W, SAMPLES), jnp.float32), (sep_upper_inv, sep_upper, sep_forward), reverse=True)
    sep_rounded = lax.optimization_barrier(sep_correction.astype(jnp.bfloat16)).astype(jnp.float32)
    before = jnp.concatenate([jnp.zeros((1, W, SAMPLES), jnp.float32), sep_rounded[:-1]], axis=0)
    upper_blocks = leaf_upper.reshape(SEPS, LEAF_DEV, 2, W, W)
    leaf_back = leaf_forward.reshape(SEPS, LEAF_DEV, W, SAMPLES)
    leaf_back = leaf_back - jnp.einsum("bmij,bjs->bmis", upper_blocks[:, :, 0].astype(jnp.float32), before)
    leaf_back = leaf_back - jnp.einsum("bmij,bjs->bmis", upper_blocks[:, :, 1].astype(jnp.float32), sep_rounded)
    back_rounded = lax.optimization_barrier(leaf_back.reshape(NLEAF, W, SAMPLES).astype(jnp.bfloat16)).astype(jnp.float32)
    leaf_correction = active_rows * jnp.einsum("lij,ljs->lis", leaf_upper_inv.astype(jnp.float32), back_rounded)
    return leaf_correction, sep_correction
```

```python
import jax
import jax.numpy as jnp
from jax import lax
from jax.sharding import Mesh
from jax.sharding import PartitionSpec as P

Z, X, C, Y = "z", "x", "c", "y"
F32, F16 = jnp.float32, jnp.float16


def exact(left_side, right_side):
    return jnp.dot(
        left_side, right_side, precision=lax.Precision.HIGHEST, preferred_element_type=F32
    )


def exponent(values, axis):
    largest = jnp.max(jnp.abs(values), axis=axis, keepdims=True)
    return jnp.clip(jnp.floor(jnp.log2(jnp.maximum(largest, 1e-36))), -120.0, 120.0)


def encode_rows(parts):
    exponents = [exponent(part, 1) for part in parts]
    scaled = [part * jnp.exp2(-k) for part, k in zip(parts, exponents)]
    room = 128 // len(parts)
    spread = [jnp.broadcast_to(k, (k.shape[0], room)) for k in exponents]
    return jnp.concatenate(scaled + spread, axis=1).astype(F16)


def decode_rows(wire, count, width):
    room = 128 // count
    start = count * width
    parts = []
    for i in range(count):
        k = wire[:, start + room * i : start + room * i + 1].astype(F32)
        parts.append(wire[:, width * i : width * (i + 1)].astype(F32) * jnp.exp2(k))
    return parts


def encode(values):
    k = exponent(values, 0)
    spread = jnp.broadcast_to(k, (16, k.shape[1]))
    return jnp.concatenate([values * jnp.exp2(-k), spread], axis=0).astype(F16)


def decode(wire):
    rows = wire.shape[1] - 16
    k = wire[:, rows : rows + 1].astype(F32)
    return wire[:, :rows].astype(F32) * jnp.exp2(k)


def to_all(block, axis):
    size = lax.axis_size(axis)
    slots = jnp.broadcast_to(block[None], (size,) + block.shape)
    return lax.all_to_all(slots, axis, 0, 0, tiled=True)


def swap_cores(block):
    return lax.ppermute(block, C, [(0, 1), (1, 0)])


def half(block, core):
    rows = block.shape[0] // 2
    return jnp.where(core == 0, block[:rows], block[rows:])


def per_device(
    leaf_rhs,
    sep_rhs,
    leaf_size,
    leaf_lower_inv,
    leaf_lower,
    leaf_upper,
    leaf_upper_inv,
    sep_lower_inv,
    sep_lower,
    sep_upper_inv,
    sep_upper,
):
    panel = (Z, X, C)
    panels = lax.axis_size(panel)
    planes, chips = lax.axis_size(Z), lax.axis_size(X)
    z, x, core = lax.axis_index(Z), lax.axis_index(X), lax.axis_index(C)
    width, samples = leaf_rhs.shape[1], leaf_rhs.shape[2]

    active_rows = (jnp.arange(width, dtype=jnp.int32)[None, :] < leaf_size[:, None]).astype(F32)[
        :, :, None
    ]
    leaf_rounded = (active_rows * leaf_rhs).astype(jnp.bfloat16)
    leaf_forward = active_rows * jnp.einsum(
        "lij,ljs->lis", leaf_lower_inv, leaf_rounded, preferred_element_type=F32
    )
    forward_rounded = leaf_forward.astype(jnp.bfloat16)
    left_terms = jnp.einsum(
        "lij,ljs->is", leaf_lower[:, 0], forward_rounded, preferred_element_type=F32
    )
    from_right = lax.ppermute(left_terms, panel, [(i + 1, i) for i in range(panels - 1)])
    own_terms = jnp.einsum(
        "lij,ljs->is", leaf_lower[:, 1], forward_rounded, preferred_element_type=F32
    )

    wire = encode_rows([sep_lower_inv[0], sep_lower[0], sep_upper_inv[0], sep_upper[0]])
    wire = to_all(wire, Y).reshape(width, -1)
    lower_inverse, lower, upper_inverse, upper = decode_rows(wire, 4, width)
    forward_factor = -exact(lower_inverse, lower)
    backward_factor = -exact(upper_inverse, upper)
    sep_source = sep_rhs[0] - own_terms - from_right
    offset = exact(lower_inverse, sep_source)

    mine = jnp.concatenate([forward_factor, backward_factor, offset], axis=1)
    other = swap_cores(mine)
    first = jnp.where(core == 0, mine, other)
    second = jnp.where(core == 0, other, mine)
    first_backward = first[:, width : 2 * width]
    pair = jnp.concatenate(
        [
            exact(second[:, :width], first[:, :width]),
            exact(first_backward, second[:, width : 2 * width]),
            second[:, 2 * width :] + exact(second[:, :width], first[:, 2 * width :]),
        ],
        axis=1,
    )
    prefix = jnp.where(core == 0, forward_factor, pair[:, :width])
    prefix_value = jnp.where(core == 0, offset, pair[:, 2 * width :])
    suffix = jnp.where(core == 0, pair[:, width : 2 * width], backward_factor)

    pairs = decode(to_all(encode(half(pair, core)), (X, C))).reshape(chips, width, -1)
    ahead = jnp.eye(width, dtype=F32)
    ahead_value = jnp.zeros((width, samples), F32)
    chip_prefix, chip_prefix_value = ahead, ahead_value
    for i in range(chips):
        factor = pairs[i, :, :width]
        ahead = factor if i == 0 else exact(factor, ahead)
        value = pairs[i, :, 2 * width :]
        ahead_value = value if i == 0 else value + exact(factor, ahead_value)
        if i < chips - 1:
            chip_prefix = jnp.where(x == i + 1, ahead, chip_prefix)
            chip_prefix_value = jnp.where(x == i + 1, ahead_value, chip_prefix_value)
    behind = jnp.eye(width, dtype=F32)
    chip_suffix = behind
    for i in range(chips - 1, -1, -1):
        factor = pairs[i, :, width : 2 * width]
        behind = factor if i == chips - 1 else exact(factor, behind)
        if i > 0:
            chip_suffix = jnp.where(x == i - 1, behind, chip_suffix)

    half_ahead, half_behind = half(ahead, core), half(behind, core)
    half_value = half(ahead_value, core)
    later = encode(jnp.concatenate([half_ahead, half_value], axis=1))
    earlier = encode(jnp.concatenate([half_behind, half_value], axis=1))
    index = jnp.arange(planes, dtype=jnp.int32)[:, None, None]
    wire = lax.all_to_all(
        jnp.where(index > z, later[None], earlier[None]), Z, 0, 0, tiled=True
    )
    wire_other = swap_cores(wire)
    first = decode(jnp.where(core == 0, wire, wire_other))
    second = decode(jnp.where(core == 0, wire_other, wire))
    all_planes = jnp.concatenate([first, second], axis=1)
    received = jnp.zeros((width, samples), F32)
    for i in range(planes - 1):
        value = all_planes[i, :, width:] + exact(all_planes[i, :, :width], received)
        received = jnp.where(z > i, value, received)
    received = chip_prefix_value + exact(chip_prefix, received)
    sep_forward = prefix_value + exact(prefix, received)

    offset = exact(upper_inverse, sep_forward)
    other = swap_cores(offset)
    first = jnp.where(core == 0, offset, other)
    second = jnp.where(core == 0, other, offset)
    pair_value = first + exact(first_backward, second)
    suffix_value = jnp.where(core == 0, pair_value, offset)
    values = decode(to_all(encode(pair_value), X))
    behind_value = jnp.zeros((width, samples), F32)
    chip_suffix_value = behind_value
    for i in range(chips - 1, -1, -1):
        factor = pairs[i, :, width : 2 * width]
        behind_value = values[i] if i == chips - 1 else values[i] + exact(factor, behind_value)
        if i > 0:
            chip_suffix_value = jnp.where(x == i - 1, behind_value, chip_suffix_value)
    values = decode(to_all(encode(behind_value), Z))
    received = jnp.zeros((width, samples), F32)
    for i in range(planes - 1, 0, -1):
        value = values[i] + exact(all_planes[i, :, :width], received)
        received = jnp.where(z < i, value, received)
    received = chip_suffix_value + exact(chip_suffix, received)
    sep_correction = suffix_value + exact(suffix, received)

    sep_rounded = sep_correction.astype(jnp.bfloat16)
    before = lax.ppermute(sep_rounded, panel, [(i, i + 1) for i in range(panels - 1)])
    leaf_back = leaf_forward - jnp.einsum(
        "lij,js->lis", leaf_upper[:, 1], sep_rounded, preferred_element_type=F32
    )
    leaf_back = leaf_back - jnp.einsum(
        "lij,js->lis", leaf_upper[:, 0], before, preferred_element_type=F32
    )
    back_rounded = leaf_back.astype(jnp.bfloat16)
    leaf_correction = active_rows * jnp.einsum(
        "lij,ljs->lis", leaf_upper_inv, back_rounded, preferred_element_type=F32
    )
    return (leaf_correction, sep_correction[None])


def solution(mesh):
    cut = Mesh(mesh.devices.reshape(8, 4, 2, 8), (Z, X, C, Y))
    panel = (Z, X, C)
    return jax.shard_map(
        per_device,
        mesh=cut,
        in_specs=(
            P(panel, None, Y),
            P(panel, None, Y),
            P(panel),
            P(panel, None, None),
            P(panel, None, None, None),
            P(panel, None, None, None),
            P(panel, None, None),
            P(panel, Y, None),
            P(panel, Y, None),
            P(panel, Y, None),
            P(panel, Y, None),
        ),
        out_specs=(P(panel, None, Y), P(panel, None, Y)),
        check_vma=False,
    )
```

```python
import functools

import jax
import jax.numpy as jnp
from jax import lax
from jax.experimental import pallas as pl
from jax.experimental.pallas import tpu as pltpu
from jax.sharding import Mesh
from jax.sharding import PartitionSpec as P

Z, X, C, Y = "z", "x", "c", "y"
F32, F16, BF16 = jnp.float32, jnp.float16, jnp.bfloat16
EXTRA = 8


def split(values):
    high = values.astype(BF16)
    return high, (values - high.astype(F32)).astype(BF16)


def product(left_side, right_side):
    left_high, left_low = split(left_side)
    right_high, right_low = split(right_side)
    rows = left_side.shape[0]
    dot = functools.partial(jnp.dot, preferred_element_type=F32)
    high = dot(jnp.concatenate([left_high, left_low], axis=0), right_high)
    return high[:rows] + (high[rows:] + dot(left_high, right_low))


def exponent(values, axis):
    largest = jnp.max(jnp.abs(values), axis=axis, keepdims=True)
    return jnp.clip(jnp.floor(jnp.log2(jnp.maximum(largest, 1e-36))), -120.0, 120.0)


def choose(condition, one, other):
    flags = jnp.zeros(one.shape, jnp.int32) + condition.astype(jnp.int32)
    return jnp.where(flags != 0, one, other)


def kernel(body, out_shapes, *operands, flops=0):
    moved = sum(o.size * o.dtype.itemsize for o in operands)
    moved += sum(o.size * o.dtype.itemsize for o in out_shapes)
    return pl.pallas_call(
        body,
        out_shape=out_shapes,
        in_specs=[
            pl.BlockSpec(memory_space=pltpu.SMEM if o.dtype == jnp.int32 else pltpu.VMEM)
            for o in operands
        ],
        out_specs=[pl.BlockSpec(memory_space=pltpu.VMEM) for _ in out_shapes],
        compiler_params=pltpu.CompilerParams(vmem_limit_bytes=16 * 2**20),
        cost_estimate=pl.CostEstimate(flops=flops, bytes_accessed=moved, transcendentals=0),
    )(*operands)


def shape(*dims, dtype=F32):
    return jax.ShapeDtypeStruct(dims, dtype)


def half_rows(core, values):
    rows = values.shape[0] // 2
    return choose(core == 0, values[:rows], values[rows:])


def half_columns(core, values):
    columns = values.shape[1] // 2
    return choose(core == 0, values[:, :columns], values[:, columns:])


def encode(wire_ref, index, values):
    rows, columns = values.shape
    k = exponent(values, 0)
    wire_ref[index + (slice(0, rows), slice(None))] = values * jnp.exp2(-k)
    wire_ref[index + (slice(rows, rows + EXTRA), slice(None))] = jnp.broadcast_to(
        k, (EXTRA, columns)
    )


def decode(ref, i, columns):
    rows = ref.shape[1] - EXTRA
    return ref[i, 0:rows, columns] * jnp.exp2(ref[i, rows : rows + 1, columns])


class Wires:
    def __init__(self, core, mine_ref, other_ref):
        self.core, self.refs = core, (mine_ref, other_ref)
        self.count = mine_ref.shape[0]
        self.width = 2 * (mine_ref.shape[1] - EXTRA)

    def in_order(self, i, columns):
        mine, other = (decode(ref, i, columns) for ref in self.refs)
        return [choose(self.core == 0, mine, other), choose(self.core == 0, other, mine)]

    def matrix(self, i, columns=None):
        columns = slice(0, self.width) if columns is None else columns
        return jnp.concatenate(self.in_order(i, columns), axis=0)

    def values(self, i, columns):
        return jnp.concatenate(self.in_order(i, columns), axis=1)

    def part(self, i, columns):
        return decode(self.refs[0], i, columns)


def pair_columns(width):
    part = width // 2
    starts = [0, width, 2 * width, 3 * width, 3 * width + part, 3 * width + 2 * part]
    return [slice(a, b) for a, b in zip(starts[:-1], starts[1:])]


def encode_rows_kernel(blocks_ref, wire_ref):
    rows, columns = blocks_ref.shape
    width = columns // 4
    exponents = []
    for i in range(4):
        values = blocks_ref[:, width * i : width * (i + 1)]
        k = exponent(values, 1)
        wire_ref[:, width * i : width * (i + 1)] = values * jnp.exp2(-k)
        exponents.append(jnp.broadcast_to(k, (rows, 128 // 4)))
    wire_ref[:, columns:] = jnp.concatenate(exponents, axis=1)


def factors_kernel(wire_ref, rhs_ref, own_ref, right_ref, out_ref, next_ref):
    width = rhs_ref.shape[0]
    room = 128 // 4

    def block(i):
        start = 4 * width + room * i
        k = wire_ref[:, start : start + 1]
        return (wire_ref[:, width * i : width * (i + 1)] * jnp.exp2(k)).T

    source = (rhs_ref[...] - own_ref[...] - right_ref[...]).T
    both = product(jnp.concatenate([-block(1), source], axis=0), block(0))
    upper_inverse = block(2)
    out_ref[0:width] = both[:width]
    backward = product(-block(3), upper_inverse)
    out_ref[width : 2 * width] = backward
    out_ref[2 * width : 3 * width] = upper_inverse
    encode(next_ref, (), jnp.concatenate([backward, upper_inverse], axis=1))
    out_ref[3 * width :] = both[width:]


def both_cores(core, mine_ref, other_ref, start, end):
    mine, other = mine_ref[start:end], other_ref[start:end]
    return choose(core == 0, mine, other), choose(core == 0, other, mine)


def pair_kernel(place_ref, mine_ref, other_ref, wire_ref):
    core = place_ref[0]
    width = mine_ref.shape[1]
    both = functools.partial(both_cores, core, mine_ref, other_ref)
    forward_first, forward_second = both(0, width)
    backward_first, backward_second = both(width, 2 * width)
    inverse_first, inverse_second = both(2 * width, 3 * width)
    offset_first, offset_second = both(3 * width, mine_ref.shape[0])
    part = width // 2
    start = jnp.concatenate([half_rows(core, forward_first), offset_first], axis=0)
    end = product(start, forward_second)
    forward, value = end[:part], end[part:] + offset_second
    back = product(jnp.concatenate([forward, value], axis=0), inverse_second)
    back = jnp.concatenate([back, half_rows(core, backward_second)], axis=0)
    back = product(back, backward_first)
    rows = start.shape[0]
    through = product(start, inverse_first) + back[:rows]
    whole = [
        forward,
        back[rows:],
        through[:part],
        half_columns(core, value),
        half_columns(core, through[part:]),
    ]
    encode(wire_ref, (), jnp.concatenate(whole, axis=1))


def plane_kernel(place_ref, first_ref, second_ref, wire_ref):
    core = place_ref[0]
    pairs = Wires(core, first_ref, second_ref)
    part = pairs.width // 2
    forward, backward, _, value, _ = pair_columns(pairs.width)
    last = pairs.count - 1
    ahead = pairs.part(0, forward)
    ahead = jnp.concatenate([ahead, pairs.values(0, value)], axis=0)
    behind = pairs.part(last, backward)
    for i in range(1, pairs.count):
        ahead = product(ahead, pairs.matrix(i, forward))
        further = ahead[part:] + pairs.values(i, value)
        ahead = jnp.concatenate([ahead[:part], further], axis=0)
        behind = product(behind, pairs.matrix(last - i, backward))
    further = half_columns(core, ahead[part:])
    encode(wire_ref, (0,), jnp.concatenate([ahead[:part], further], axis=1))
    encode(wire_ref, (1,), jnp.concatenate([behind, further], axis=1))


def forward_kernel(
    place_ref, plane_first, plane_second, pair_first, pair_second, wire_ref, through_ref, start_ref
):
    core, x, z = place_ref[0], place_ref[1], place_ref[2]
    planes, pairs = Wires(core, plane_first, plane_second), Wires(core, pair_first, pair_second)
    width = pairs.width
    forward, backward, through, value, back_value = pair_columns(width)
    received = jnp.zeros(start_ref.shape, F32)
    for i in range(planes.count - 1):
        further = planes.values(i, slice(width, None)) + product(received, planes.matrix(i))
        received = choose(z > i, further, received)
    ahead = []
    for i in range(pairs.count):
        ahead.append(received)
        if i < pairs.count - 1:
            received = pairs.values(i, value) + product(received, pairs.matrix(i, forward))
    behind = None
    for i in range(pairs.count - 1, -1, -1):
        own = pairs.values(i, back_value) + product(ahead[i], pairs.matrix(i, through))
        through_ref[i] = own
        if behind is not None:
            own = own + product(behind, pairs.matrix(i, backward))
        behind = own
    encode(wire_ref, (), half_columns(core, behind))
    start = ahead[0]
    for i in range(1, pairs.count):
        start = choose(x == i, ahead[i], start)
    start_ref[...] = start


def values_kernel(
    place_ref, start_ref, mine_ref, other_ref, previous_ref, first_ref, second_ref, before_ref
):
    core = place_ref[0]
    width = mine_ref.shape[1]
    start = start_ref[...]
    both = functools.partial(both_cores, core, mine_ref, other_ref)
    factor_first, factor_second = both(0, width)
    inverse_first, inverse_second = both(2 * width, 3 * width)
    offset_first, offset_second = both(3 * width, mine_ref.shape[0])
    forward_first = offset_first + product(start, factor_first)
    forward_second = offset_second + product(forward_first, factor_second)
    first_ref[...] = product(forward_first, inverse_first)
    second_ref[...] = product(forward_second, inverse_second)
    before_ref[...] = product(start, decode_previous(previous_ref, slice(width, None)))


def decode_previous(ref, columns):
    rows = ref.shape[0] - EXTRA
    return ref[0:rows, columns] * jnp.exp2(ref[rows : rows + 1, columns])


def backward_kernel(
    place_ref, size_ref, value_first, value_second, plane_first, plane_second,
    pair_first, pair_second, through_ref, mine_ref, other_ref, first_ref, second_ref, before_ref,
    previous_ref, leaf_forward_ref, leaf_upper_ref, leaf_upper_inv_ref, leaf_ref, sep_ref,
):
    core, x, z = place_ref[0], place_ref[1], place_ref[2]
    planes, pairs = Wires(core, plane_first, plane_second), Wires(core, pair_first, pair_second)
    values = Wires(core, value_first, value_second)
    width = pairs.width
    backward = pair_columns(width)[1]
    received = jnp.zeros(first_ref.shape, F32)
    for i in range(planes.count - 1, 0, -1):
        further = values.values(i, slice(None)) + product(received, planes.matrix(i))
        received = choose(z < i, further, received)
    chip = received
    for i in range(pairs.count - 1, 0, -1):
        received = through_ref[i] + product(received, pairs.matrix(i, backward))
        chip = choose(x < i, received, chip)
    factor_first, factor_second = both_cores(core, mine_ref, other_ref, width, 2 * width)
    second = second_ref[...] + product(chip, factor_second)
    first = first_ref[...] + product(second, factor_first)
    before = before_ref[...] + product(first, decode_previous(previous_ref, slice(0, width)))
    sep = choose(core == 0, first, second).T
    before = choose(core == 0, before, first).T.astype(BF16)
    sep_ref[...] = sep
    sep = sep.astype(BF16)
    dot = functools.partial(jnp.dot, preferred_element_type=F32)
    rows = lax.broadcasted_iota(jnp.int32, sep.shape, 0)
    for leaf in range(leaf_ref.shape[0]):
        back = leaf_forward_ref[leaf] - dot(leaf_upper_ref[leaf, 0], before)
        back = back - dot(leaf_upper_ref[leaf, 1], sep)
        result = dot(leaf_upper_inv_ref[leaf], back.astype(BF16))
        leaf_ref[leaf] = jnp.where(rows < size_ref[leaf], result, 0.0)


def to_all(block, axis):
    size = lax.axis_size(axis)
    slots = jnp.broadcast_to(block.astype(F16)[None], (size,) + block.shape)
    return lax.all_to_all(slots, axis, 0, 0, tiled=True)


def swap_cores(block):
    return lax.ppermute(block, C, [(0, 1), (1, 0)])


def in_order(core, block):
    other = swap_cores(block)
    return block.astype(F32), other.astype(F32)


def per_device(
    leaf_rhs,
    sep_rhs,
    leaf_size,
    leaf_lower_inv,
    leaf_lower,
    leaf_upper,
    leaf_upper_inv,
    sep_lower_inv,
    sep_lower,
    sep_upper_inv,
    sep_upper,
):
    panel = (Z, X, C)
    panels = lax.axis_size(panel)
    planes, chips = lax.axis_size(Z), lax.axis_size(X)
    z, x, core = lax.axis_index(Z), lax.axis_index(X), lax.axis_index(C)
    place = jnp.stack([core, x, z]).astype(jnp.int32)
    leaves, width, samples = leaf_rhs.shape

    blocks = [sep_lower_inv[0], sep_lower[0], sep_upper_inv[0], sep_upper[0]]
    blocks = jnp.concatenate(blocks, axis=1)
    (wire,) = kernel(
        encode_rows_kernel, [shape(blocks.shape[0], blocks.shape[1] + 128)], blocks
    )
    wire = to_all(wire, Y).reshape(width, -1).astype(F32)

    active_rows = (jnp.arange(width, dtype=jnp.int32)[None, :] < leaf_size[:, None]).astype(F32)[
        :, :, None
    ]
    leaf_rounded = (active_rows * leaf_rhs).astype(BF16)
    leaf_forward = active_rows * jnp.einsum(
        "lij,ljs->lis", leaf_lower_inv, leaf_rounded, preferred_element_type=F32
    )
    forward_rounded = leaf_forward.astype(BF16)
    left_terms = jnp.einsum(
        "lij,ljs->is", leaf_lower[:, 0], forward_rounded, preferred_element_type=F32
    )
    from_right = lax.ppermute(left_terms, panel, [(i + 1, i) for i in range(panels - 1)])
    own_terms = jnp.einsum(
        "lij,ljs->is", leaf_lower[:, 1], forward_rounded, preferred_element_type=F32
    )

    mine, previous = kernel(
        factors_kernel,
        [shape(3 * width + samples, width), shape(width + EXTRA, 2 * width)],
        wire,
        sep_rhs[0],
        own_terms,
        from_right,
    )
    other = swap_cores(mine)
    to_next_chip = [(i, i + 1) for i in range(1, panels - 1, 2)]
    previous = lax.ppermute(previous.astype(F16), panel, to_next_chip)
    rows = width // 2 + EXTRA
    (wire,) = kernel(pair_kernel, [shape(rows, 4 * width)], place, mine, other)

    wire, previous = lax.optimization_barrier((wire.astype(F16), previous))
    pairs = in_order(core, to_all(wire, X))
    previous = previous.astype(F32)
    (wire,) = kernel(plane_kernel, [shape(2, rows, width + width // 2)], place, *pairs)

    wire = wire.astype(F16)
    index = jnp.arange(planes, dtype=jnp.int32)[:, None, None]
    slots = jnp.where(index > z, wire[0][None], wire[1][None])
    between = in_order(core, lax.all_to_all(slots, Z, 0, 0, tiled=True))
    block = shape(samples, width)
    wire, through, start = kernel(
        forward_kernel,
        [shape(rows, width // 2), shape(chips, samples, width), block],
        place,
        *between,
        *pairs,
    )
    values = in_order(core, to_all(wire, Z))
    first, second, before = kernel(
        values_kernel, [block, block, block], place, start, mine, other, previous
    )

    leaf_correction, sep_correction = kernel(
        backward_kernel,
        [shape(leaves, width, samples), shape(width, samples)],
        place,
        leaf_size,
        *values,
        *between,
        *pairs,
        through,
        mine,
        other,
        first,
        second,
        before,
        previous,
        leaf_forward,
        leaf_upper,
        leaf_upper_inv,
    )
    return (leaf_correction, sep_correction[None])


def solution(mesh):
    cut = Mesh(mesh.devices.reshape(8, 4, 2, 8), (Z, X, C, Y))
    panel = (Z, X, C)
    return jax.shard_map(
        per_device,
        mesh=cut,
        in_specs=(
            P(panel, None, Y),
            P(panel, None, Y),
            P(panel),
            P(panel, None, None),
            P(panel, None, None, None),
            P(panel, None, None, None),
            P(panel, None, None),
            P(panel, Y, None),
            P(panel, Y, None),
            P(panel, Y, None),
            P(panel, Y, None),
        ),
        out_specs=(P(panel, None, Y), P(panel, None, Y)),
        check_vma=False,
    )
```

```python
import functools

import jax
import jax.numpy as jnp
from jax import lax
from jax.experimental import pallas as pl
from jax.experimental.pallas import tpu as pltpu
from jax.sharding import Mesh
from jax.sharding import PartitionSpec as P

Z, X, C, Y = "z", "x", "c", "y"
F32, F16, BF16 = jnp.float32, jnp.float16, jnp.bfloat16
LANES, EXTRA = 128, 8


def split(values):
    high = values.astype(BF16)
    return high, (values - high.astype(F32)).astype(BF16)


def product(left_side, right_side):
    left_high, left_low = split(left_side)
    right_high, right_low = split(right_side)
    rows = left_side.shape[0]
    dot = functools.partial(jnp.dot, preferred_element_type=F32)
    high = dot(jnp.concatenate([left_high, left_low], axis=0), right_high)
    return high[:rows] + (high[rows:] + dot(left_high, right_low))


def exponent(values, axis):
    largest = jnp.max(jnp.abs(values), axis=axis, keepdims=True)
    return jnp.clip(jnp.floor(jnp.log2(jnp.maximum(largest, 1e-36))), -120.0, 120.0)


def choose(condition, one, other):
    flags = jnp.zeros(one.shape, jnp.int32) + condition.astype(jnp.int32)
    return jnp.where(flags != 0, one, other)


def kernel(body, out_shapes, *operands, flops=0):
    moved = sum(o.size * o.dtype.itemsize for o in operands)
    moved += sum(o.size * o.dtype.itemsize for o in out_shapes)
    return pl.pallas_call(
        body,
        out_shape=out_shapes,
        in_specs=[
            pl.BlockSpec(memory_space=pltpu.SMEM if o.dtype == jnp.int32 else pltpu.VMEM)
            for o in operands
        ],
        out_specs=[pl.BlockSpec(memory_space=pltpu.VMEM) for _ in out_shapes],
        compiler_params=pltpu.CompilerParams(vmem_limit_bytes=16 * 2**20),
        cost_estimate=pl.CostEstimate(flops=flops, bytes_accessed=moved, transcendentals=0),
    )(*operands)


def shape(*dims, dtype=F32):
    return jax.ShapeDtypeStruct(dims, dtype)


def half_rows(core, values):
    rows = values.shape[0] // 2
    return choose(core == 0, values[:rows], values[rows:])


def half_columns(core, values):
    columns = values.shape[1] // 2
    return choose(core == 0, values[:, :columns], values[:, columns:])


def wire_shape(*dims):
    *outer, rows, columns = dims
    return shape(*outer, columns // LANES * rows + EXTRA, LANES)


def encode(wire_ref, index, values):
    rows, columns = values.shape
    k = exponent(values, 0)
    scaled = values * jnp.exp2(-k)
    count = columns // LANES
    wire_ref[index + (slice(count * rows, None),)] = jnp.zeros((EXTRA, LANES), F32)
    for b in range(count):
        block = slice(LANES * b, LANES * (b + 1))
        wire_ref[index + (slice(rows * b, rows * (b + 1)),)] = scaled[:, block]
        wire_ref[index + (slice(count * rows + b, count * rows + b + 1),)] = k[:, block]


def decode(ref, index, rows, columns):
    count = (ref.shape[-2] - EXTRA) // rows
    blocks = []
    for b in range(columns.start // LANES, columns.stop // LANES):
        k = ref[index + (slice(count * rows + b, count * rows + b + 1),)]
        blocks.append(ref[index + (slice(rows * b, rows * (b + 1)),)] * jnp.exp2(k))
    return jnp.concatenate(blocks, axis=1)


class Wires:
    def __init__(self, core, mine_ref, other_ref):
        self.core, self.refs = core, (mine_ref, other_ref)
        self.count, self.part = mine_ref.shape[0], mine_ref.shape[2]
        self.width = 2 * self.part

    def in_order(self, i, columns):
        mine, other = (decode(ref, (i,), self.part, columns) for ref in self.refs)
        return [choose(self.core == 0, mine, other), choose(self.core == 0, other, mine)]

    def matrix(self, i, columns=None):
        columns = slice(0, self.width) if columns is None else columns
        return jnp.concatenate(self.in_order(i, columns), axis=0)

    def values(self, i, columns):
        return jnp.concatenate(self.in_order(i, columns), axis=1)

    def own_part(self, i, columns):
        return decode(self.refs[0], (i,), self.part, columns)


def pair_columns(width):
    part = width // 2
    starts = [0, width, 2 * width, 3 * width, 3 * width + part, 3 * width + 2 * part]
    return [slice(a, b) for a, b in zip(starts[:-1], starts[1:])]


def encode_rows_kernel(blocks_ref, wire_ref):
    encode(wire_ref, (), blocks_ref[...])


def factors_kernel(wire_ref, rhs_ref, own_ref, right_ref, out_ref, next_ref):
    width = rhs_ref.shape[0]
    senders = wire_ref.shape[0]

    def block(i):
        columns = slice(width * i, width * (i + 1))
        rows = [decode(wire_ref, (j,), width // senders, columns) for j in range(senders)]
        return jnp.concatenate(rows, axis=0).T

    source = (rhs_ref[...] - own_ref[...] - right_ref[...]).T
    both = product(jnp.concatenate([-block(1), source], axis=0), block(0))
    upper_inverse = block(2)
    out_ref[0:width] = both[:width]
    backward = product(-block(3), upper_inverse)
    out_ref[width : 2 * width] = backward
    out_ref[2 * width : 3 * width] = upper_inverse
    encode(next_ref, (), jnp.concatenate([backward, upper_inverse], axis=1))
    out_ref[3 * width :] = both[width:]


def both_cores(core, mine_ref, other_ref, start, end):
    mine, other = mine_ref[start:end], other_ref[start:end]
    return choose(core == 0, mine, other), choose(core == 0, other, mine)


def pair_kernel(place_ref, mine_ref, other_ref, wire_ref):
    core = place_ref[0]
    width = mine_ref.shape[1]
    both = functools.partial(both_cores, core, mine_ref, other_ref)
    forward_first, forward_second = both(0, width)
    backward_first, backward_second = both(width, 2 * width)
    inverse_first, inverse_second = both(2 * width, 3 * width)
    offset_first, offset_second = both(3 * width, mine_ref.shape[0])
    part = width // 2
    start = jnp.concatenate([half_rows(core, forward_first), offset_first], axis=0)
    end = product(start, forward_second)
    forward, value = end[:part], end[part:] + offset_second
    back = product(jnp.concatenate([forward, value], axis=0), inverse_second)
    back = jnp.concatenate([back, half_rows(core, backward_second)], axis=0)
    back = product(back, backward_first)
    rows = start.shape[0]
    through = product(start, inverse_first) + back[:rows]
    whole = [
        forward,
        back[rows:],
        through[:part],
        half_columns(core, value),
        half_columns(core, through[part:]),
    ]
    encode(wire_ref, (), jnp.concatenate(whole, axis=1))


def plane_kernel(place_ref, first_ref, second_ref, wire_ref):
    core = place_ref[0]
    pairs = Wires(core, first_ref, second_ref)
    part = pairs.width // 2
    forward, backward, _, value, _ = pair_columns(pairs.width)
    last = pairs.count - 1
    ahead = pairs.own_part(0, forward)
    ahead = jnp.concatenate([ahead, pairs.values(0, value)], axis=0)
    behind = pairs.own_part(last, backward)
    for i in range(1, pairs.count):
        ahead = product(ahead, pairs.matrix(i, forward))
        further = ahead[part:] + pairs.values(i, value)
        ahead = jnp.concatenate([ahead[:part], further], axis=0)
        behind = product(behind, pairs.matrix(last - i, backward))
    further = half_columns(core, ahead[part:])
    encode(wire_ref, (0,), jnp.concatenate([ahead[:part], further], axis=1))
    encode(wire_ref, (1,), jnp.concatenate([behind, further], axis=1))


def through_kernel(place_ref, mine_ref, other_ref, factor_ref, value_ref):
    pairs = Wires(place_ref[0], mine_ref, other_ref)
    width = pairs.width
    forward, backward, through, value, back_value = pair_columns(width)

    def add_value(block, further):
        return jnp.concatenate([block[:width], block[width:] + further], axis=0)

    ahead = jnp.concatenate([pairs.matrix(0, forward), pairs.values(0, value)], axis=0)
    own = [jnp.concatenate([pairs.matrix(0, through), pairs.values(0, back_value)], axis=0)]
    for i in range(1, pairs.count):
        further = product(ahead, pairs.matrix(i, through))
        own.append(add_value(further, pairs.values(i, back_value)))
        if i < pairs.count - 1:
            further = product(ahead, pairs.matrix(i, forward))
            ahead = add_value(further, pairs.values(i, value))
    behind = own[-1]
    for i in range(pairs.count - 2, -1, -1):
        behind = own[i] + product(behind, pairs.matrix(i, backward))
    factor_ref[...] = behind[:width]
    value_ref[...] = behind[width:]


def forward_kernel(
    place_ref, plane_mine, plane_other, factor_ref, value_ref, wire_ref, ahead_ref
):
    core, z = place_ref[0], place_ref[2]
    planes = Wires(core, plane_mine, plane_other)
    width = planes.width
    received = jnp.zeros(ahead_ref.shape, F32)
    for i in range(planes.count - 1):
        offset = planes.values(i, slice(width, width + planes.part))
        received = choose(z > i, offset + product(received, planes.matrix(i)), received)
    ahead_ref[...] = received
    behind = value_ref[...] + product(received, factor_ref[...])
    encode(wire_ref, (), half_columns(core, behind))


def values_kernel(
    place_ref, ahead_ref, pair_mine, pair_other, mine_ref, other_ref, previous_ref,
    through_ref, first_ref, second_ref, before_ref,
):
    core, x = place_ref[0], place_ref[1]
    pairs = Wires(core, pair_mine, pair_other)
    width = pairs.width
    forward, _, through, value, back_value = pair_columns(width)
    ahead = ahead_ref[...]
    start = ahead
    through_ref[0] = jnp.zeros(ahead.shape, F32)
    for i in range(1, pairs.count):
        ahead = pairs.values(i - 1, value) + product(ahead, pairs.matrix(i - 1, forward))
        start = choose(x == i, ahead, start)
        through_ref[i] = pairs.values(i, back_value) + product(ahead, pairs.matrix(i, through))
    both = functools.partial(both_cores, core, mine_ref, other_ref)
    factor_first, factor_second = both(0, width)
    inverse_first, inverse_second = both(2 * width, 3 * width)
    offset_first, offset_second = both(3 * width, mine_ref.shape[0])
    forward_first = offset_first + product(start, factor_first)
    forward_second = offset_second + product(forward_first, factor_second)
    first_ref[...] = product(forward_first, inverse_first)
    second_ref[...] = product(forward_second, inverse_second)
    previous = decode(previous_ref, (), width, slice(width, 2 * width))
    before_ref[...] = product(start, previous)


def backward_kernel(
    place_ref, size_ref, value_first, value_second, plane_first, plane_second,
    pair_first, pair_second, through_ref, mine_ref, other_ref, first_ref, second_ref, before_ref,
    previous_ref, leaf_forward_ref, leaf_upper_ref, leaf_upper_inv_ref, leaf_ref, sep_ref,
):
    core, x, z = place_ref[0], place_ref[1], place_ref[2]
    planes, pairs = Wires(core, plane_first, plane_second), Wires(core, pair_first, pair_second)
    values = Wires(core, value_first, value_second)
    width = pairs.width
    backward = pair_columns(width)[1]
    received = jnp.zeros(first_ref.shape, F32)
    for i in range(planes.count - 1, 0, -1):
        further = values.values(i, slice(0, values.part)) + product(received, planes.matrix(i))
        received = choose(z < i, further, received)
    chip = received
    for i in range(pairs.count - 1, 0, -1):
        received = through_ref[i] + product(received, pairs.matrix(i, backward))
        chip = choose(x < i, received, chip)
    factor_first, factor_second = both_cores(core, mine_ref, other_ref, width, 2 * width)
    second = second_ref[...] + product(chip, factor_second)
    first = first_ref[...] + product(second, factor_first)
    previous = decode(previous_ref, (), width, slice(0, width))
    before = before_ref[...] + product(first, previous)
    sep = choose(core == 0, first, second).T
    before = choose(core == 0, before, first).T.astype(BF16)
    sep_ref[...] = sep
    sep = sep.astype(BF16)
    dot = functools.partial(jnp.dot, preferred_element_type=F32)
    rows = lax.broadcasted_iota(jnp.int32, sep.shape, 0)
    for leaf in range(leaf_ref.shape[0]):
        back = leaf_forward_ref[leaf] - dot(leaf_upper_ref[leaf, 0], before)
        back = back - dot(leaf_upper_ref[leaf, 1], sep)
        result = dot(leaf_upper_inv_ref[leaf], back.astype(BF16))
        leaf_ref[leaf] = jnp.where(rows < size_ref[leaf], result, 0.0)


def to_all(block, axis):
    size = lax.axis_size(axis)
    slots = jnp.broadcast_to(block.astype(F16)[None], (size,) + block.shape)
    return lax.all_to_all(slots, axis, 0, 0, tiled=True)


def swap_cores(block):
    return lax.ppermute(block, C, [(0, 1), (1, 0)])


def in_order(core, block):
    other = swap_cores(block)
    return block.astype(F32), other.astype(F32)


def per_device(
    leaf_rhs,
    sep_rhs,
    leaf_size,
    leaf_lower_inv,
    leaf_lower,
    leaf_upper,
    leaf_upper_inv,
    sep_lower_inv,
    sep_lower,
    sep_upper_inv,
    sep_upper,
):
    panel = (Z, X, C)
    panels = lax.axis_size(panel)
    planes, chips = lax.axis_size(Z), lax.axis_size(X)
    z, x, core = lax.axis_index(Z), lax.axis_index(X), lax.axis_index(C)
    place = jnp.stack([core, x, z]).astype(jnp.int32)
    leaves, width, samples = leaf_rhs.shape

    blocks = [sep_lower_inv[0], sep_lower[0], sep_upper_inv[0], sep_upper[0]]
    blocks = jnp.concatenate(blocks, axis=1)
    (wire,) = kernel(
        encode_rows_kernel, [wire_shape(*blocks.shape)], blocks
    )
    wire = to_all(wire, Y).astype(F32)

    active_rows = (jnp.arange(width, dtype=jnp.int32)[None, :] < leaf_size[:, None]).astype(F32)[
        :, :, None
    ]
    leaf_rounded = (active_rows * leaf_rhs).astype(BF16)
    leaf_forward = active_rows * jnp.einsum(
        "lij,ljs->lis", leaf_lower_inv, leaf_rounded, preferred_element_type=F32
    )
    forward_rounded = leaf_forward.astype(BF16)
    left_terms = jnp.einsum(
        "lij,ljs->is", leaf_lower[:, 0], forward_rounded, preferred_element_type=F32
    )
    from_right = lax.ppermute(left_terms, panel, [(i + 1, i) for i in range(panels - 1)])
    own_terms = jnp.einsum(
        "lij,ljs->is", leaf_lower[:, 1], forward_rounded, preferred_element_type=F32
    )

    mine, previous = kernel(
        factors_kernel,
        [shape(3 * width + samples, width), wire_shape(width, 2 * width)],
        wire,
        sep_rhs[0],
        own_terms,
        from_right,
    )
    other = swap_cores(mine)
    to_next_chip = [(i, i + 1) for i in range(1, panels - 1, 2)]
    previous = lax.ppermute(previous.astype(F16), panel, to_next_chip)
    part = width // 2
    (wire,) = kernel(pair_kernel, [wire_shape(part, 4 * width)], place, mine, other)

    wire, previous = lax.optimization_barrier((wire.astype(F16), previous))
    pairs = in_order(core, to_all(wire, X))
    previous = previous.astype(F32)
    (wire,) = kernel(plane_kernel, [wire_shape(2, part, width + part)], place, *pairs)

    wire = wire.astype(F16)
    index = jnp.arange(planes, dtype=jnp.int32)[:, None, None]
    slots = jnp.where(index > z, wire[0][None], wire[1][None])
    between = in_order(core, lax.all_to_all(slots, Z, 0, 0, tiled=True))
    block = shape(samples, width)
    through = kernel(
        through_kernel, [shape(width, width), shape(samples, width)], place, *pairs
    )
    wire, ahead = kernel(
        forward_kernel, [wire_shape(part, part), block], place, *between, *through
    )
    values = in_order(core, to_all(wire, Z))
    through, first, second, before = kernel(
        values_kernel,
        [shape(chips, samples, width), block, block, block],
        place,
        ahead,
        *pairs,
        mine,
        other,
        previous,
    )

    leaf_correction, sep_correction = kernel(
        backward_kernel,
        [shape(leaves, width, samples), shape(width, samples)],
        place,
        leaf_size,
        *values,
        *between,
        *pairs,
        through,
        mine,
        other,
        first,
        second,
        before,
        previous,
        leaf_forward,
        leaf_upper,
        leaf_upper_inv,
    )
    return (leaf_correction, sep_correction[None])


def solution(mesh):
    cut = Mesh(mesh.devices.reshape(8, 4, 2, 8), (Z, X, C, Y))
    panel = (Z, X, C)
    return jax.shard_map(
        per_device,
        mesh=cut,
        in_specs=(
            P(panel, None, Y),
            P(panel, None, Y),
            P(panel),
            P(panel, None, None),
            P(panel, None, None, None),
            P(panel, None, None, None),
            P(panel, None, None),
            P(panel, Y, None),
            P(panel, Y, None),
            P(panel, Y, None),
            P(panel, Y, None),
        ),
        out_specs=(P(panel, None, Y), P(panel, None, Y)),
        check_vma=False,
    )
```

```python
import functools

import jax
import jax.numpy as jnp
from jax import lax
from jax.experimental import pallas as pl
from jax.experimental.pallas import tpu as pltpu
from jax.sharding import Mesh
from jax.sharding import PartitionSpec as P

Z, X, C, Y = "z", "x", "c", "y"
F32, F16, BF16 = jnp.float32, jnp.float16, jnp.bfloat16
LANES, EXTRA = 128, 8


def split(values):
    high = values.astype(BF16)
    return high, (values - high.astype(F32)).astype(BF16)


def product(left_side, right_side):
    left_high, left_low = split(left_side)
    right_high, right_low = split(right_side)
    rows = left_side.shape[0]
    dot = functools.partial(jnp.dot, preferred_element_type=F32)
    high = dot(jnp.concatenate([left_high, left_low], axis=0), right_high)
    return high[:rows] + (high[rows:] + dot(left_high, right_low))


def exponent(values, axis):
    largest = jnp.max(jnp.abs(values), axis=axis, keepdims=True)
    return jnp.clip(jnp.floor(jnp.log2(jnp.maximum(largest, 1e-36))), -120.0, 120.0)


def choose(condition, one, other):
    flags = jnp.zeros(one.shape, jnp.int32) + condition.astype(jnp.int32)
    return jnp.where(flags != 0, one, other)


def kernel(body, out_shapes, *operands, left_in_hbm=(), scratch=(), flops=0):
    moved = sum(o.size * o.dtype.itemsize for o in operands)
    moved += sum(o.size * o.dtype.itemsize for o in out_shapes)
    return pl.pallas_call(
        body,
        out_shape=out_shapes,
        in_specs=[
            pl.BlockSpec(memory_space=pltpu.SMEM if o.dtype == jnp.int32 else pltpu.VMEM)
            for o in operands
        ]
        + [pl.BlockSpec(memory_space=pltpu.HBM) for _ in left_in_hbm],
        out_specs=[pl.BlockSpec(memory_space=pltpu.VMEM) for _ in out_shapes],
        scratch_shapes=scratch,
        compiler_params=pltpu.CompilerParams(vmem_limit_bytes=16 * 2**20),
        cost_estimate=pl.CostEstimate(flops=flops, bytes_accessed=moved, transcendentals=0),
    )(*operands, *left_in_hbm)


def shape(*dims, dtype=F32):
    return jax.ShapeDtypeStruct(dims, dtype)


def half_rows(core, values):
    rows = values.shape[0] // 2
    return choose(core == 0, values[:rows], values[rows:])


def half_columns(core, values):
    columns = values.shape[1] // 2
    return choose(core == 0, values[:, :columns], values[:, columns:])


def wire_shape(*dims):
    *outer, rows, columns = dims
    return shape(*outer, columns // LANES * rows + EXTRA, LANES)


def encode(wire_ref, index, values):
    rows, columns = values.shape
    k = exponent(values, 0)
    scaled = values * jnp.exp2(-k)
    count = columns // LANES
    wire_ref[index + (slice(count * rows, None),)] = jnp.zeros((EXTRA, LANES), F32)
    for b in range(count):
        block = slice(LANES * b, LANES * (b + 1))
        wire_ref[index + (slice(rows * b, rows * (b + 1)),)] = scaled[:, block]
        wire_ref[index + (slice(count * rows + b, count * rows + b + 1),)] = k[:, block]


def decode(ref, index, rows, columns):
    count = (ref.shape[-2] - EXTRA) // rows
    blocks = []
    for b in range(columns.start // LANES, columns.stop // LANES):
        k = ref[index + (slice(count * rows + b, count * rows + b + 1),)]
        blocks.append(ref[index + (slice(rows * b, rows * (b + 1)),)] * jnp.exp2(k))
    return jnp.concatenate(blocks, axis=1)


class Wires:
    def __init__(self, core, mine_ref, other_ref):
        self.core, self.refs = core, (mine_ref, other_ref)
        self.count, self.part = mine_ref.shape[0], mine_ref.shape[2]
        self.width = 2 * self.part

    def in_order(self, i, columns):
        mine, other = (decode(ref, (i,), self.part, columns) for ref in self.refs)
        return [choose(self.core == 0, mine, other), choose(self.core == 0, other, mine)]

    def matrix(self, i, columns=None):
        columns = slice(0, self.width) if columns is None else columns
        return jnp.concatenate(self.in_order(i, columns), axis=0)

    def values(self, i, columns):
        return jnp.concatenate(self.in_order(i, columns), axis=1)

    def own_part(self, i, columns):
        return decode(self.refs[0], (i,), self.part, columns)


def pair_columns(width):
    part = width // 2
    starts = [0, width, 2 * width, 3 * width, 3 * width + part, 3 * width + 2 * part]
    return [slice(a, b) for a, b in zip(starts[:-1], starts[1:])]


def encode_rows_kernel(blocks_ref, wire_ref):
    encode(wire_ref, (), blocks_ref[...])


def factors_kernel(wire_ref, rhs_ref, own_ref, right_ref, out_ref, next_ref):
    width = rhs_ref.shape[0]
    senders = wire_ref.shape[0]

    def block(i):
        columns = slice(width * i, width * (i + 1))
        rows = [decode(wire_ref, (j,), width // senders, columns) for j in range(senders)]
        return jnp.concatenate(rows, axis=0).T

    source = (rhs_ref[...] - own_ref[...] - right_ref[...]).T
    both = product(jnp.concatenate([-block(1), source], axis=0), block(0))
    upper_inverse = block(2)
    out_ref[0:width] = both[:width]
    backward = product(-block(3), upper_inverse)
    out_ref[width : 2 * width] = backward
    out_ref[2 * width : 3 * width] = upper_inverse
    encode(next_ref, (), jnp.concatenate([backward, upper_inverse], axis=1))
    out_ref[3 * width :] = both[width:]


def both_cores(core, mine_ref, other_ref, start, end):
    mine, other = mine_ref[start:end], other_ref[start:end]
    return choose(core == 0, mine, other), choose(core == 0, other, mine)


def pair_kernel(place_ref, mine_ref, other_ref, wire_ref):
    core = place_ref[0]
    width = mine_ref.shape[1]
    both = functools.partial(both_cores, core, mine_ref, other_ref)
    forward_first, forward_second = both(0, width)
    backward_first, backward_second = both(width, 2 * width)
    inverse_first, inverse_second = both(2 * width, 3 * width)
    offset_first, offset_second = both(3 * width, mine_ref.shape[0])
    part = width // 2
    start = jnp.concatenate([half_rows(core, forward_first), offset_first], axis=0)
    end = product(start, forward_second)
    forward, value = end[:part], end[part:] + offset_second
    back = product(jnp.concatenate([forward, value], axis=0), inverse_second)
    back = jnp.concatenate([back, half_rows(core, backward_second)], axis=0)
    back = product(back, backward_first)
    rows = start.shape[0]
    through = product(start, inverse_first) + back[:rows]
    whole = [
        forward,
        back[rows:],
        through[:part],
        half_columns(core, value),
        half_columns(core, through[part:]),
    ]
    encode(wire_ref, (), jnp.concatenate(whole, axis=1))


def plane_kernel(place_ref, first_ref, second_ref, wire_ref):
    core = place_ref[0]
    pairs = Wires(core, first_ref, second_ref)
    part = pairs.width // 2
    forward, backward, _, value, _ = pair_columns(pairs.width)
    last = pairs.count - 1
    ahead = pairs.own_part(0, forward)
    ahead = jnp.concatenate([ahead, pairs.values(0, value)], axis=0)
    behind = pairs.own_part(last, backward)
    for i in range(1, pairs.count):
        ahead = product(ahead, pairs.matrix(i, forward))
        further = ahead[part:] + pairs.values(i, value)
        ahead = jnp.concatenate([ahead[:part], further], axis=0)
        behind = product(behind, pairs.matrix(last - i, backward))
    further = half_columns(core, ahead[part:])
    encode(wire_ref, (0,), jnp.concatenate([ahead[:part], further], axis=1))
    encode(wire_ref, (1,), jnp.concatenate([behind, further], axis=1))


def through_kernel(place_ref, mine_ref, other_ref, factor_ref, value_ref, start_ref, own_ref):
    x = place_ref[1]
    pairs = Wires(place_ref[0], mine_ref, other_ref)
    width = pairs.width
    forward, backward, through, value, back_value = pair_columns(width)

    def add_value(block, further):
        return jnp.concatenate([block[:width], block[width:] + further], axis=0)

    ahead = jnp.concatenate([pairs.matrix(0, forward), pairs.values(0, value)], axis=0)
    own = [jnp.concatenate([pairs.matrix(0, through), pairs.values(0, back_value)], axis=0)]
    start = ahead
    for i in range(1, pairs.count):
        start = choose(x == i, ahead, start)
        further = product(ahead, pairs.matrix(i, through))
        own.append(add_value(further, pairs.values(i, back_value)))
        if i < pairs.count - 1:
            further = product(ahead, pairs.matrix(i, forward))
            ahead = add_value(further, pairs.values(i, value))
    start_ref[...] = start
    for i in range(pairs.count):
        own_ref[i] = own[i]
    behind = own[-1]
    for i in range(pairs.count - 2, -1, -1):
        factor, offset = pairs.matrix(i, backward), own[i]
        if i == 0:
            factor, offset = half_columns(pairs.core, factor), half_columns(pairs.core, offset)
        behind = offset + product(behind, factor)
    factor_ref[...] = behind[:width]
    value_ref[...] = behind[width:]


def forward_kernel(
    place_ref, plane_mine, plane_other, factor_ref, value_ref, wire_ref, ahead_ref
):
    core, z = place_ref[0], place_ref[2]
    planes = Wires(core, plane_mine, plane_other)
    width = planes.width
    received = jnp.zeros(ahead_ref.shape, F32)
    for i in range(planes.count - 1):
        further = planes.values(i, slice(width, width + planes.part))
        if i > 0:
            further = further + product(received, planes.matrix(i))
        received = choose(z > i, further, received)
    ahead_ref[...] = received
    behind = value_ref[...] + product(received, factor_ref[...])
    wire_ref[...] = behind.astype(BF16)


def values_kernel(
    place_ref, ahead_ref, start_factor_ref, own_ref, mine_ref, other_ref, previous_ref,
    through_ref, first_ref, second_ref, before_ref,
):
    core, x = place_ref[0], place_ref[1]
    width = mine_ref.shape[1]
    ahead = ahead_ref[...]
    start = start_factor_ref[width:] + product(ahead, start_factor_ref[:width])
    start = choose(x == 0, ahead, start)
    through_ref[0] = jnp.zeros(ahead.shape, F32)
    for i in range(1, own_ref.shape[0]):
        through_ref[i] = own_ref[i, width:] + product(ahead, own_ref[i, :width])
    both = functools.partial(both_cores, core, mine_ref, other_ref)
    factor_first, factor_second = both(0, width)
    inverse_first, inverse_second = both(2 * width, 3 * width)
    offset_first, offset_second = both(3 * width, mine_ref.shape[0])
    forward_first = offset_first + product(start, factor_first)
    forward_second = offset_second + product(forward_first, factor_second)
    first_ref[...] = product(forward_first, inverse_first)
    second_ref[...] = product(forward_second, inverse_second)
    previous = decode(previous_ref, (), width, slice(width, 2 * width))
    before_ref[...] = product(start, previous)


def backward_kernel(
    place_ref, size_ref, value_first, value_second, plane_first, plane_second,
    pair_first, pair_second, through_ref, mine_ref, other_ref, first_ref, second_ref, before_ref,
    previous_ref, leaf_forward_ref, far_upper_ref, far_upper_inv_ref, leaf_ref, sep_ref,
    leaf_upper_ref, leaf_upper_inv_ref, arrived,
):
    copies = [
        pltpu.make_async_copy(far_upper_ref, leaf_upper_ref, arrived.at[0]),
        pltpu.make_async_copy(far_upper_inv_ref, leaf_upper_inv_ref, arrived.at[1]),
    ]
    for copy in copies:
        copy.start()
    core, x, z = place_ref[0], place_ref[1], place_ref[2]
    planes, pairs = Wires(core, plane_first, plane_second), Wires(core, pair_first, pair_second)
    width = pairs.width
    backward = pair_columns(width)[1]
    received = jnp.zeros(first_ref.shape, F32)
    for i in range(planes.count - 1, 0, -1):
        mine, other = value_first[i].astype(F32), value_second[i].astype(F32)
        offset = [choose(core == 0, mine, other), choose(core == 0, other, mine)]
        further = jnp.concatenate(offset, axis=1)
        if i < planes.count - 1:
            further = further + product(received, planes.matrix(i))
        received = choose(z < i, further, received)
    chip = received
    for i in range(pairs.count - 1, 0, -1):
        received = through_ref[i] + product(received, pairs.matrix(i, backward))
        chip = choose(x < i, received, chip)
    factor_first, factor_second = both_cores(core, mine_ref, other_ref, width, 2 * width)
    second = second_ref[...] + product(chip, factor_second)
    first = first_ref[...] + product(second, factor_first)
    previous = decode(previous_ref, (), width, slice(0, width))
    before = before_ref[...] + product(first, previous)
    sep = choose(core == 0, first, second).T
    before = choose(core == 0, before, first).T.astype(BF16)
    sep_ref[...] = sep
    sep = sep.astype(BF16)
    dot = functools.partial(jnp.dot, preferred_element_type=F32)
    rows = lax.broadcasted_iota(jnp.int32, sep.shape, 0)
    for copy in copies:
        copy.wait()
    for leaf in range(leaf_ref.shape[0]):
        back = leaf_forward_ref[leaf] - dot(leaf_upper_ref[leaf, 0], before)
        back = back - dot(leaf_upper_ref[leaf, 1], sep)
        result = dot(leaf_upper_inv_ref[leaf], back.astype(BF16))
        leaf_ref[leaf] = jnp.where(rows < size_ref[leaf], result, 0.0)


def to_all(block, axis, dtype=F16):
    size = lax.axis_size(axis)
    slots = jnp.broadcast_to(block.astype(dtype)[None], (size,) + block.shape)
    return lax.all_to_all(slots, axis, 0, 0, tiled=True)


def swap_cores(block):
    return lax.ppermute(block, C, [(0, 1), (1, 0)])


def in_order(core, block):
    other = swap_cores(block)
    return block.astype(F32), other.astype(F32)


def per_device(
    leaf_rhs,
    sep_rhs,
    leaf_size,
    leaf_lower_inv,
    leaf_lower,
    leaf_upper,
    leaf_upper_inv,
    sep_lower_inv,
    sep_lower,
    sep_upper_inv,
    sep_upper,
):
    panel = (Z, X, C)
    panels = lax.axis_size(panel)
    planes, chips = lax.axis_size(Z), lax.axis_size(X)
    z, x, core = lax.axis_index(Z), lax.axis_index(X), lax.axis_index(C)
    place = jnp.stack([core, x, z]).astype(jnp.int32)
    leaves, width, samples = leaf_rhs.shape

    blocks = [sep_lower_inv[0], sep_lower[0], sep_upper_inv[0], sep_upper[0]]
    blocks = jnp.concatenate(blocks, axis=1)
    (wire,) = kernel(
        encode_rows_kernel, [wire_shape(*blocks.shape)], blocks
    )
    wire = to_all(wire, Y).astype(F32)

    active_rows = (jnp.arange(width, dtype=jnp.int32)[None, :] < leaf_size[:, None]).astype(F32)[
        :, :, None
    ]
    leaf_rounded = (active_rows * leaf_rhs).astype(BF16)
    leaf_forward = active_rows * jnp.einsum(
        "lij,ljs->lis", leaf_lower_inv, leaf_rounded, preferred_element_type=F32
    )
    forward_rounded = leaf_forward.astype(BF16)
    left_terms = jnp.einsum(
        "lij,ljs->is", leaf_lower[:, 0], forward_rounded, preferred_element_type=F32
    )
    from_right = lax.ppermute(left_terms, panel, [(i + 1, i) for i in range(panels - 1)])
    own_terms = jnp.einsum(
        "lij,ljs->is", leaf_lower[:, 1], forward_rounded, preferred_element_type=F32
    )

    mine, previous = kernel(
        factors_kernel,
        [shape(3 * width + samples, width), wire_shape(width, 2 * width)],
        wire,
        sep_rhs[0],
        own_terms,
        from_right,
    )
    other = swap_cores(mine)
    to_next_chip = [(i, i + 1) for i in range(1, panels - 1, 2)]
    previous = lax.ppermute(previous.astype(F16), panel, to_next_chip)
    part = width // 2
    (wire,) = kernel(pair_kernel, [wire_shape(part, 4 * width)], place, mine, other)

    wire, previous = lax.optimization_barrier((wire.astype(F16), previous))
    pairs = in_order(core, to_all(wire, X))
    previous = previous.astype(F32)
    (wire,) = kernel(plane_kernel, [wire_shape(2, part, width + part)], place, *pairs)

    wire = wire.astype(F16)
    index = jnp.arange(planes, dtype=jnp.int32)[:, None, None]
    slots = jnp.where(index > z, wire[0][None], wire[1][None])
    between = in_order(core, lax.all_to_all(slots, Z, 0, 0, tiled=True))
    block = shape(samples, width)
    *through, start, own = kernel(
        through_kernel,
        [
            shape(width, part),
            shape(samples, part),
            shape(width + samples, width),
            shape(chips, width + samples, width),
        ],
        place,
        *pairs,
    )
    wire, ahead = kernel(
        forward_kernel, [shape(samples, part, dtype=BF16), block], place, *between, *through
    )
    values = to_all(wire, Z, BF16)
    values = values, swap_cores(values)
    through, first, second, before = kernel(
        values_kernel,
        [shape(chips, samples, width), block, block, block],
        place,
        ahead,
        start,
        own,
        mine,
        other,
        previous,
    )

    leaf_correction, sep_correction = kernel(
        backward_kernel,
        [shape(leaves, width, samples), shape(width, samples)],
        place,
        leaf_size,
        *values,
        *between,
        *pairs,
        through,
        mine,
        other,
        first,
        second,
        before,
        previous,
        leaf_forward,
        left_in_hbm=[leaf_upper, leaf_upper_inv],
        scratch=[
            pltpu.VMEM(leaf_upper.shape, BF16),
            pltpu.VMEM(leaf_upper_inv.shape, BF16),
            pltpu.SemaphoreType.DMA((2,)),
        ],
    )
    return (leaf_correction, sep_correction[None])


def solution(mesh):
    cut = Mesh(mesh.devices.reshape(8, 4, 2, 8), (Z, X, C, Y))
    panel = (Z, X, C)
    return jax.shard_map(
        per_device,
        mesh=cut,
        in_specs=(
            P(panel, None, Y),
            P(panel, None, Y),
            P(panel),
            P(panel, None, None),
            P(panel, None, None, None),
            P(panel, None, None, None),
            P(panel, None, None),
            P(panel, Y, None),
            P(panel, Y, None),
            P(panel, Y, None),
            P(panel, Y, None),
        ),
        out_specs=(P(panel, None, Y), P(panel, None, Y)),
        check_vma=False,
    )
```

```python
import functools

import jax
import jax.numpy as jnp
from jax import lax
from jax.experimental import pallas as pl
from jax.experimental.pallas import tpu as pltpu
from jax.sharding import Mesh
from jax.sharding import PartitionSpec as P

Z, X, C, Y = "z", "x", "c", "y"
F32, F16, BF16 = jnp.float32, jnp.float16, jnp.bfloat16
LANES, EXTRA = 128, 8


def split(values):
    high = values.astype(BF16)
    return high, (values - high.astype(F32)).astype(BF16)


def product(left_side, right_side):
    left_high, left_low = split(left_side)
    right_high, right_low = split(right_side)
    rows = left_side.shape[0]
    dot = functools.partial(jnp.dot, preferred_element_type=F32)
    high = dot(jnp.concatenate([left_high, left_low], axis=0), right_high)
    return high[:rows] + (high[rows:] + dot(left_high, right_low))


def exponent(values, axis):
    largest = jnp.max(jnp.abs(values), axis=axis, keepdims=True)
    return jnp.clip(jnp.floor(jnp.log2(jnp.maximum(largest, 1e-36))), -120.0, 120.0)


def choose(condition, one, other):
    flags = jnp.zeros(one.shape, jnp.int32) + condition.astype(jnp.int32)
    return jnp.where(flags != 0, one, other)


def kernel(body, out_shapes, *operands, left_in_hbm=(), scratch=(), flops=0):
    moved = sum(o.size * o.dtype.itemsize for o in operands)
    moved += sum(o.size * o.dtype.itemsize for o in out_shapes)
    return pl.pallas_call(
        body,
        out_shape=out_shapes,
        in_specs=[
            pl.BlockSpec(memory_space=pltpu.SMEM if o.dtype == jnp.int32 else pltpu.VMEM)
            for o in operands
        ]
        + [pl.BlockSpec(memory_space=pltpu.HBM) for _ in left_in_hbm],
        out_specs=[pl.BlockSpec(memory_space=pltpu.VMEM) for _ in out_shapes],
        scratch_shapes=scratch,
        compiler_params=pltpu.CompilerParams(vmem_limit_bytes=16 * 2**20),
        cost_estimate=pl.CostEstimate(flops=flops, bytes_accessed=moved, transcendentals=0),
    )(*operands, *left_in_hbm)


def shape(*dims, dtype=F32):
    return jax.ShapeDtypeStruct(dims, dtype)


def half_rows(core, values):
    rows = values.shape[0] // 2
    return choose(core == 0, values[:rows], values[rows:])


def half_columns(core, values):
    columns = values.shape[1] // 2
    return choose(core == 0, values[:, :columns], values[:, columns:])


def wire_shape(*dims):
    *outer, rows, columns = dims
    return shape(*outer, columns // LANES * rows + EXTRA, LANES)


def encode(wire_ref, index, values):
    rows, columns = values.shape
    k = exponent(values, 0)
    scaled = values * jnp.exp2(-k)
    count = columns // LANES
    wire_ref[index + (slice(count * rows, None),)] = jnp.zeros((EXTRA, LANES), F32)
    for b in range(count):
        block = slice(LANES * b, LANES * (b + 1))
        wire_ref[index + (slice(rows * b, rows * (b + 1)),)] = scaled[:, block]
        wire_ref[index + (slice(count * rows + b, count * rows + b + 1),)] = k[:, block]


def decode(ref, index, rows, columns):
    count = (ref.shape[-2] - EXTRA) // rows
    blocks = []
    for b in range(columns.start // LANES, columns.stop // LANES):
        k = ref[index + (slice(count * rows + b, count * rows + b + 1),)]
        blocks.append(ref[index + (slice(rows * b, rows * (b + 1)),)] * jnp.exp2(k))
    return jnp.concatenate(blocks, axis=1)


class Wires:
    def __init__(self, core, mine_ref, other_ref):
        self.core, self.refs = core, (mine_ref, other_ref)
        self.count, self.part = mine_ref.shape[0], mine_ref.shape[2]
        self.width = 2 * self.part

    def in_order(self, i, columns):
        mine, other = (decode(ref, (i,), self.part, columns) for ref in self.refs)
        return [choose(self.core == 0, mine, other), choose(self.core == 0, other, mine)]

    def matrix(self, i, columns=None):
        columns = slice(0, self.width) if columns is None else columns
        return jnp.concatenate(self.in_order(i, columns), axis=0)

    def values(self, i, columns):
        return jnp.concatenate(self.in_order(i, columns), axis=1)

    def own_part(self, i, columns):
        return decode(self.refs[0], (i,), self.part, columns)


def pair_columns(width):
    part = width // 2
    starts = [0, width, 2 * width, 3 * width, 3 * width + part, 3 * width + 2 * part]
    return [slice(a, b) for a, b in zip(starts[:-1], starts[1:])]


def encode_rows_kernel(blocks_ref, wire_ref):
    encode(wire_ref, (), blocks_ref[...])


def factors_kernel(wire_ref, rhs_ref, own_ref, right_ref, out_ref, next_ref):
    width = rhs_ref.shape[0]
    senders = wire_ref.shape[0]

    def block(i):
        columns = slice(width * i, width * (i + 1))
        rows = [decode(wire_ref, (j,), width // senders, columns) for j in range(senders)]
        return jnp.concatenate(rows, axis=0).T

    source = (rhs_ref[...] - own_ref[...] - right_ref[...]).T
    both = product(jnp.concatenate([-block(1), source], axis=0), block(0))
    upper_inverse = block(2)
    out_ref[0:width] = both[:width]
    backward = product(-block(3), upper_inverse)
    out_ref[width : 2 * width] = backward
    out_ref[2 * width : 3 * width] = upper_inverse
    encode(next_ref, (), jnp.concatenate([backward, upper_inverse], axis=1))
    out_ref[3 * width :] = both[width:]


def both_cores(core, mine_ref, other_ref, start, end):
    mine, other = mine_ref[start:end], other_ref[start:end]
    return choose(core == 0, mine, other), choose(core == 0, other, mine)


def pair_kernel(place_ref, mine_ref, other_ref, wire_ref):
    core = place_ref[0]
    width = mine_ref.shape[1]
    both = functools.partial(both_cores, core, mine_ref, other_ref)
    forward_first, forward_second = both(0, width)
    backward_first, backward_second = both(width, 2 * width)
    inverse_first, inverse_second = both(2 * width, 3 * width)
    offset_first, offset_second = both(3 * width, mine_ref.shape[0])
    part = width // 2
    start = jnp.concatenate([half_rows(core, forward_first), offset_first], axis=0)
    end = product(start, forward_second)
    forward, value = end[:part], end[part:] + offset_second
    back = product(jnp.concatenate([forward, value], axis=0), inverse_second)
    back = jnp.concatenate([back, half_rows(core, backward_second)], axis=0)
    back = product(back, backward_first)
    rows = start.shape[0]
    through = product(start, inverse_first) + back[:rows]
    whole = [
        forward,
        back[rows:],
        through[:part],
        half_columns(core, value),
        half_columns(core, through[part:]),
    ]
    encode(wire_ref, (), jnp.concatenate(whole, axis=1))


def plane_kernel(place_ref, first_ref, second_ref, wire_ref):
    core = place_ref[0]
    pairs = Wires(core, first_ref, second_ref)
    part = pairs.width // 2
    forward, backward, _, value, _ = pair_columns(pairs.width)
    last = pairs.count - 1
    ahead = pairs.own_part(0, forward)
    ahead = jnp.concatenate([ahead, pairs.values(0, value)], axis=0)
    behind = pairs.own_part(last, backward)
    for i in range(1, pairs.count):
        ahead = product(ahead, pairs.matrix(i, forward))
        further = ahead[part:] + pairs.values(i, value)
        ahead = jnp.concatenate([ahead[:part], further], axis=0)
        behind = product(behind, pairs.matrix(last - i, backward))
    further = half_columns(core, ahead[part:])
    encode(wire_ref, (0,), jnp.concatenate([ahead[:part], further], axis=1))
    encode(wire_ref, (1,), jnp.concatenate([behind, further], axis=1))


def through_kernel(place_ref, mine_ref, other_ref, factor_ref, value_ref, start_ref, own_ref):
    x = place_ref[1]
    pairs = Wires(place_ref[0], mine_ref, other_ref)
    width = pairs.width
    forward, backward, through, value, back_value = pair_columns(width)

    def add_value(block, further):
        return jnp.concatenate([block[:width], block[width:] + further], axis=0)

    ahead = jnp.concatenate([pairs.matrix(0, forward), pairs.values(0, value)], axis=0)
    own = [jnp.concatenate([pairs.matrix(0, through), pairs.values(0, back_value)], axis=0)]
    start = ahead
    for i in range(1, pairs.count):
        start = choose(x == i, ahead, start)
        further = product(ahead, pairs.matrix(i, through))
        own.append(add_value(further, pairs.values(i, back_value)))
        if i < pairs.count - 1:
            further = product(ahead, pairs.matrix(i, forward))
            ahead = add_value(further, pairs.values(i, value))
    start_ref[...] = start
    for i in range(pairs.count):
        own_ref[i] = own[i]
    behind = own[-1]
    for i in range(pairs.count - 2, -1, -1):
        factor, offset = pairs.matrix(i, backward), own[i]
        if i == 0:
            factor, offset = half_columns(pairs.core, factor), half_columns(pairs.core, offset)
        behind = offset + product(behind, factor)
    factor_ref[...] = behind[:width]
    value_ref[...] = behind[width:]


def forward_kernel(
    place_ref, plane_mine, plane_other, factor_ref, value_ref, wire_ref, ahead_ref
):
    core, z = place_ref[0], place_ref[2]
    planes = Wires(core, plane_mine, plane_other)
    width = planes.width
    received = jnp.zeros(ahead_ref.shape, F32)
    for i in range(planes.count - 1):
        further = planes.values(i, slice(width, width + planes.part))
        if i > 0:
            further = further + product(received, planes.matrix(i))
        received = choose(z > i, further, received)
    ahead_ref[...] = received
    behind = value_ref[...] + product(received, factor_ref[...])
    wire_ref[...] = behind.astype(BF16)


def values_kernel(
    place_ref, ahead_ref, start_factor_ref, own_ref, mine_ref, other_ref, previous_ref,
    through_ref, first_ref, second_ref, before_ref,
):
    core, x = place_ref[0], place_ref[1]
    width = mine_ref.shape[1]
    ahead = ahead_ref[...]
    start = start_factor_ref[width:] + product(ahead, start_factor_ref[:width])
    start = choose(x == 0, ahead, start)
    through_ref[0] = jnp.zeros(ahead.shape, F32)
    for i in range(1, own_ref.shape[0]):
        through_ref[i] = own_ref[i, width:] + product(ahead, own_ref[i, :width])
    both = functools.partial(both_cores, core, mine_ref, other_ref)
    factor_first, factor_second = both(0, width)
    inverse_first, inverse_second = both(2 * width, 3 * width)
    offset_first, offset_second = both(3 * width, mine_ref.shape[0])
    forward_first = offset_first + product(start, factor_first)
    forward_second = offset_second + product(forward_first, factor_second)
    first_ref[...] = product(forward_first, inverse_first)
    second_ref[...] = product(forward_second, inverse_second)
    previous = decode(previous_ref, (), width, slice(width, 2 * width))
    before_ref[...] = product(start, previous)


def backward_kernel(
    place_ref, size_ref, value_first, value_second, plane_first, plane_second,
    pair_first, pair_second, through_ref, mine_ref, other_ref, first_ref, second_ref, before_ref,
    previous_ref, leaf_forward_ref, far_upper_ref, far_upper_inv_ref, leaf_ref, sep_ref,
    leaf_upper_ref, leaf_upper_inv_ref, arrived,
):
    copies = [
        pltpu.make_async_copy(far_upper_ref, leaf_upper_ref, arrived.at[0]),
        pltpu.make_async_copy(far_upper_inv_ref, leaf_upper_inv_ref, arrived.at[1]),
    ]
    for copy in copies:
        copy.start()
    core, x, z = place_ref[0], place_ref[1], place_ref[2]
    planes, pairs = Wires(core, plane_first, plane_second), Wires(core, pair_first, pair_second)
    width = pairs.width
    backward = pair_columns(width)[1]
    received = jnp.zeros(first_ref.shape, F32)
    for i in range(planes.count - 1, 0, -1):
        mine, other = value_first[i].astype(F32), value_second[i].astype(F32)
        offset = [choose(core == 0, mine, other), choose(core == 0, other, mine)]
        further = jnp.concatenate(offset, axis=1)
        if i < planes.count - 1:
            further = further + product(received, planes.matrix(i))
        received = choose(z < i, further, received)
    chip = received
    for i in range(pairs.count - 1, 0, -1):
        received = through_ref[i] + product(received, pairs.matrix(i, backward))
        chip = choose(x < i, received, chip)
    factor_first, factor_second = both_cores(core, mine_ref, other_ref, width, 2 * width)
    second = second_ref[...] + product(chip, factor_second)
    first = first_ref[...] + product(second, factor_first)
    previous = decode(previous_ref, (), width, slice(0, width))
    before = before_ref[...] + product(first, previous)
    sep = choose(core == 0, first, second).T
    before = choose(core == 0, before, first).T.astype(BF16)
    sep_ref[...] = sep
    sep = sep.astype(BF16)
    dot = functools.partial(jnp.dot, preferred_element_type=F32)
    rows = lax.broadcasted_iota(jnp.int32, sep.shape, 0)
    for copy in copies:
        copy.wait()
    for leaf in range(leaf_ref.shape[0]):
        back = leaf_forward_ref[leaf] - dot(leaf_upper_ref[leaf, 0], before)
        back = back - dot(leaf_upper_ref[leaf, 1], sep)
        result = dot(leaf_upper_inv_ref[leaf], back.astype(BF16))
        leaf_ref[leaf] = jnp.where(rows < size_ref[leaf], result, 0.0)


def to_all(block, axis, dtype=F16):
    size = lax.axis_size(axis)
    slots = jnp.broadcast_to(block.astype(dtype)[None], (size,) + block.shape)
    return lax.all_to_all(slots, axis, 0, 0, tiled=True)


def swap_cores(block):
    return lax.ppermute(block, C, [(0, 1), (1, 0)])


def in_order(core, block):
    other = swap_cores(block)
    return block.astype(F32), other.astype(F32)


def per_device(
    leaf_rhs,
    sep_rhs,
    leaf_size,
    leaf_lower_inv,
    leaf_lower,
    leaf_upper,
    leaf_upper_inv,
    sep_lower_inv,
    sep_lower,
    sep_upper_inv,
    sep_upper,
):
    panel = (Z, X, C)
    panels = lax.axis_size(panel)
    planes, chips = lax.axis_size(Z), lax.axis_size(X)
    z, x, core = lax.axis_index(Z), lax.axis_index(X), lax.axis_index(C)
    place = jnp.stack([core, x, z]).astype(jnp.int32)
    leaves, width, samples = leaf_rhs.shape

    blocks = [sep_lower_inv[0], sep_lower[0], sep_upper_inv[0], sep_upper[0]]
    blocks = jnp.concatenate(blocks, axis=1)
    (wire,) = kernel(
        encode_rows_kernel, [wire_shape(*blocks.shape)], blocks
    )
    wire = to_all(wire, Y).astype(F32)

    active_rows = (jnp.arange(width, dtype=jnp.int32)[None, :] < leaf_size[:, None]).astype(F32)[
        :, :, None
    ]
    leaf_rounded = (active_rows * leaf_rhs).astype(BF16)
    leaf_forward = active_rows * jnp.einsum(
        "lij,ljs->lis", leaf_lower_inv, leaf_rounded, preferred_element_type=F32
    )
    forward_rounded = leaf_forward.astype(BF16)
    left_terms = jnp.einsum(
        "lij,ljs->is", leaf_lower[:, 0], forward_rounded, preferred_element_type=F32
    )
    from_right = lax.ppermute(left_terms, panel, [(i + 1, i) for i in range(panels - 1)])
    own_terms = jnp.einsum(
        "lij,ljs->is", leaf_lower[:, 1], forward_rounded, preferred_element_type=F32
    )

    mine, previous = kernel(
        factors_kernel,
        [shape(3 * width + samples, width), wire_shape(width, 2 * width)],
        wire,
        sep_rhs[0],
        own_terms,
        from_right,
    )
    other = swap_cores(mine)
    to_next_chip = [(i, i + 1) for i in range(1, panels - 1, 2)]
    previous = lax.ppermute(previous.astype(F16), panel, to_next_chip)
    part = width // 2
    (wire,) = kernel(pair_kernel, [wire_shape(part, 4 * width)], place, mine, other)

    pairs = in_order(core, to_all(wire, X))
    (wire,) = kernel(plane_kernel, [wire_shape(2, part, width + part)], place, *pairs)

    wire, previous = lax.optimization_barrier((wire.astype(F16), previous))
    previous = previous.astype(F32)
    index = jnp.arange(planes, dtype=jnp.int32)[:, None, None]
    slots = jnp.where(index > z, wire[0][None], wire[1][None])
    between = in_order(core, lax.all_to_all(slots, Z, 0, 0, tiled=True))
    block = shape(samples, width)
    *through, start, own = kernel(
        through_kernel,
        [
            shape(width, part),
            shape(samples, part),
            shape(width + samples, width),
            shape(chips, width + samples, width),
        ],
        place,
        *pairs,
    )
    wire, ahead = kernel(
        forward_kernel, [shape(samples, part, dtype=BF16), block], place, *between, *through
    )
    values = to_all(wire, Z, BF16)
    values = values, swap_cores(values)
    through, first, second, before = kernel(
        values_kernel,
        [shape(chips, samples, width), block, block, block],
        place,
        ahead,
        start,
        own,
        mine,
        other,
        previous,
    )

    leaf_correction, sep_correction = kernel(
        backward_kernel,
        [shape(leaves, width, samples), shape(width, samples)],
        place,
        leaf_size,
        *values,
        *between,
        *pairs,
        through,
        mine,
        other,
        first,
        second,
        before,
        previous,
        leaf_forward,
        left_in_hbm=[leaf_upper, leaf_upper_inv],
        scratch=[
            pltpu.VMEM(leaf_upper.shape, BF16),
            pltpu.VMEM(leaf_upper_inv.shape, BF16),
            pltpu.SemaphoreType.DMA((2,)),
        ],
    )
    return (leaf_correction, sep_correction[None])


def solution(mesh):
    cut = Mesh(mesh.devices.reshape(8, 4, 2, 8), (Z, X, C, Y))
    panel = (Z, X, C)
    return jax.shard_map(
        per_device,
        mesh=cut,
        in_specs=(
            P(panel, None, Y),
            P(panel, None, Y),
            P(panel),
            P(panel, None, None),
            P(panel, None, None, None),
            P(panel, None, None, None),
            P(panel, None, None),
            P(panel, Y, None),
            P(panel, Y, None),
            P(panel, Y, None),
            P(panel, Y, None),
        ),
        out_specs=(P(panel, None, Y), P(panel, None, Y)),
        check_vma=False,
    )
```

```python
import functools

import jax
import jax.numpy as jnp
from jax import lax
from jax.experimental import pallas as pl
from jax.experimental.pallas import tpu as pltpu
from jax.sharding import Mesh
from jax.sharding import PartitionSpec as P

Z, X, C, Y = "z", "x", "c", "y"
F32, F16, BF16 = jnp.float32, jnp.float16, jnp.bfloat16
LANES, EXTRA = 128, 8


def split(values):
    high = values.astype(BF16)
    return high, (values - high.astype(F32)).astype(BF16)


def product(left_side, right_side):
    left_high, left_low = split(left_side)
    right_high, right_low = split(right_side)
    rows = left_side.shape[0]
    dot = functools.partial(jnp.dot, preferred_element_type=F32)
    high = dot(jnp.concatenate([left_high, left_low], axis=0), right_high)
    return high[:rows] + (high[rows:] + dot(left_high, right_low))


def exponent(values, axis):
    largest = jnp.max(jnp.abs(values), axis=axis, keepdims=True)
    return jnp.clip(jnp.floor(jnp.log2(jnp.maximum(largest, 1e-36))), -120.0, 120.0)


def choose(condition, one, other):
    flags = jnp.zeros(one.shape, jnp.int32) + condition.astype(jnp.int32)
    return jnp.where(flags != 0, one, other)


def kernel(body, out_shapes, *operands, left_in_hbm=(), scratch=(), flops=0):
    moved = sum(o.size * o.dtype.itemsize for o in operands)
    moved += sum(o.size * o.dtype.itemsize for o in out_shapes)
    return pl.pallas_call(
        body,
        out_shape=out_shapes,
        in_specs=[
            pl.BlockSpec(memory_space=pltpu.SMEM if o.dtype == jnp.int32 else pltpu.VMEM)
            for o in operands
        ]
        + [pl.BlockSpec(memory_space=pltpu.HBM) for _ in left_in_hbm],
        out_specs=[pl.BlockSpec(memory_space=pltpu.VMEM) for _ in out_shapes],
        scratch_shapes=scratch,
        compiler_params=pltpu.CompilerParams(vmem_limit_bytes=16 * 2**20),
        cost_estimate=pl.CostEstimate(flops=flops, bytes_accessed=moved, transcendentals=0),
    )(*operands, *left_in_hbm)


def shape(*dims, dtype=F32):
    return jax.ShapeDtypeStruct(dims, dtype)


def half_rows(core, values):
    rows = values.shape[0] // 2
    return choose(core == 0, values[:rows], values[rows:])


def half_columns(core, values):
    columns = values.shape[1] // 2
    return choose(core == 0, values[:, :columns], values[:, columns:])


def wire_shape(*dims):
    *outer, rows, columns = dims
    return shape(*outer, columns // LANES * rows + EXTRA, LANES)


def encode(wire_ref, index, values):
    rows, columns = values.shape
    k = exponent(values, 0)
    scaled = values * jnp.exp2(-k)
    count = columns // LANES
    wire_ref[index + (slice(count * rows, None),)] = jnp.zeros((EXTRA, LANES), F32)
    for b in range(count):
        block = slice(LANES * b, LANES * (b + 1))
        wire_ref[index + (slice(rows * b, rows * (b + 1)),)] = scaled[:, block]
        wire_ref[index + (slice(count * rows + b, count * rows + b + 1),)] = k[:, block]


def decode(ref, index, rows, columns):
    count = (ref.shape[-2] - EXTRA) // rows
    blocks = []
    for b in range(columns.start // LANES, columns.stop // LANES):
        k = ref[index + (slice(count * rows + b, count * rows + b + 1),)]
        blocks.append(ref[index + (slice(rows * b, rows * (b + 1)),)] * jnp.exp2(k))
    return jnp.concatenate(blocks, axis=1)


class Wires:
    def __init__(self, core, mine_ref, other_ref):
        self.core, self.refs = core, (mine_ref, other_ref)
        self.count, self.part = mine_ref.shape[0], mine_ref.shape[2]
        self.width = 2 * self.part

    def in_order(self, i, columns):
        mine, other = (decode(ref, (i,), self.part, columns) for ref in self.refs)
        return [choose(self.core == 0, mine, other), choose(self.core == 0, other, mine)]

    def matrix(self, i, columns=None):
        columns = slice(0, self.width) if columns is None else columns
        return jnp.concatenate(self.in_order(i, columns), axis=0)

    def values(self, i, columns):
        return jnp.concatenate(self.in_order(i, columns), axis=1)

    def own_part(self, i, columns):
        return decode(self.refs[0], (i,), self.part, columns)


def pair_columns(width):
    part = width // 2
    starts = [0, width, 2 * width, 3 * width, 3 * width + part, 3 * width + 2 * part]
    return [slice(a, b) for a, b in zip(starts[:-1], starts[1:])]


def encode_rows_kernel(blocks_ref, wire_ref):
    encode(wire_ref, (), blocks_ref[...])


def factors_kernel(wire_ref, rhs_ref, own_ref, right_ref, out_ref, next_ref):
    width = rhs_ref.shape[0]
    senders = wire_ref.shape[0]

    def block(i):
        columns = slice(width * i, width * (i + 1))
        rows = [decode(wire_ref, (j,), width // senders, columns) for j in range(senders)]
        return jnp.concatenate(rows, axis=0).T

    source = (rhs_ref[...] - own_ref[...] - right_ref[...]).T
    both = product(jnp.concatenate([-block(1), source], axis=0), block(0))
    upper_inverse = block(2)
    out_ref[0:width] = both[:width]
    backward = product(-block(3), upper_inverse)
    out_ref[width : 2 * width] = backward
    out_ref[2 * width : 3 * width] = upper_inverse
    encode(next_ref, (), jnp.concatenate([backward, upper_inverse], axis=1))
    out_ref[3 * width :] = both[width:]


def both_cores(core, mine_ref, other_ref, start, end):
    mine, other = mine_ref[start:end], other_ref[start:end]
    return choose(core == 0, mine, other), choose(core == 0, other, mine)


def pair_kernel(place_ref, mine_ref, other_ref, wire_ref):
    core = place_ref[0]
    width = mine_ref.shape[1]
    both = functools.partial(both_cores, core, mine_ref, other_ref)
    forward_first, forward_second = both(0, width)
    backward_first, backward_second = both(width, 2 * width)
    inverse_first, inverse_second = both(2 * width, 3 * width)
    offset_first, offset_second = both(3 * width, mine_ref.shape[0])
    part = width // 2
    start = jnp.concatenate([half_rows(core, forward_first), offset_first], axis=0)
    end = product(start, forward_second)
    forward, value = end[:part], end[part:] + offset_second
    back = product(jnp.concatenate([forward, value], axis=0), inverse_second)
    back = jnp.concatenate([back, half_rows(core, backward_second)], axis=0)
    back = product(back, backward_first)
    rows = start.shape[0]
    through = product(start, inverse_first) + back[:rows]
    whole = [
        forward,
        back[rows:],
        through[:part],
        half_columns(core, value),
        half_columns(core, through[part:]),
    ]
    encode(wire_ref, (), jnp.concatenate(whole, axis=1))


def plane_kernel(place_ref, first_ref, second_ref, wire_ref):
    core = place_ref[0]
    pairs = Wires(core, first_ref, second_ref)
    part = pairs.width // 2
    forward, backward, _, value, _ = pair_columns(pairs.width)
    last = pairs.count - 1
    ahead = pairs.own_part(0, forward)
    ahead = jnp.concatenate([ahead, pairs.values(0, value)], axis=0)
    behind = pairs.own_part(last, backward)
    for i in range(1, pairs.count):
        ahead = product(ahead, pairs.matrix(i, forward))
        further = ahead[part:] + pairs.values(i, value)
        ahead = jnp.concatenate([ahead[:part], further], axis=0)
        behind = product(behind, pairs.matrix(last - i, backward))
    further = half_columns(core, ahead[part:])
    encode(wire_ref, (0,), jnp.concatenate([ahead[:part], further], axis=1))
    encode(wire_ref, (1,), jnp.concatenate([behind, further], axis=1))


def through_kernel(place_ref, mine_ref, other_ref, start_ref, own_ref):
    x = place_ref[1]
    pairs = Wires(place_ref[0], mine_ref, other_ref)
    width = pairs.width
    forward, _, through, value, back_value = pair_columns(width)

    def add_value(block, further):
        return jnp.concatenate([block[:width], block[width:] + further], axis=0)

    ahead = jnp.concatenate([pairs.matrix(0, forward), pairs.values(0, value)], axis=0)
    own = [jnp.concatenate([pairs.matrix(0, through), pairs.values(0, back_value)], axis=0)]
    start = ahead
    for i in range(1, pairs.count):
        start = choose(x == i, ahead, start)
        further = product(ahead, pairs.matrix(i, through))
        own.append(add_value(further, pairs.values(i, back_value)))
        if i < pairs.count - 1:
            further = product(ahead, pairs.matrix(i, forward))
            ahead = add_value(further, pairs.values(i, value))
    start_ref[...] = start
    for i in range(pairs.count):
        own_ref[i] = own[i]


def compose_kernel(place_ref, mine_ref, other_ref, own_ref, factor_ref, value_ref):
    pairs = Wires(place_ref[0], mine_ref, other_ref)
    width = pairs.width
    backward = pair_columns(width)[1]
    behind = own_ref[pairs.count - 1]
    for i in range(pairs.count - 2, -1, -1):
        factor, offset = pairs.matrix(i, backward), own_ref[i]
        if i == 0:
            factor, offset = half_columns(pairs.core, factor), half_columns(pairs.core, offset)
        behind = offset + product(behind, factor)
    factor_ref[...] = behind[:width]
    value_ref[...] = behind[width:]


def forward_kernel(
    place_ref, plane_mine, plane_other, factor_ref, value_ref, wire_ref, ahead_ref
):
    core, z = place_ref[0], place_ref[2]
    planes = Wires(core, plane_mine, plane_other)
    width = planes.width
    received = jnp.zeros(ahead_ref.shape, F32)
    for i in range(planes.count - 1):
        further = planes.values(i, slice(width, width + planes.part))
        if i > 0:
            further = further + product(received, planes.matrix(i))
        received = choose(z > i, further, received)
    ahead_ref[...] = received
    behind = value_ref[...] + product(received, factor_ref[...])
    wire_ref[...] = behind.astype(BF16)


def values_kernel(
    place_ref, ahead_ref, start_factor_ref, own_ref, mine_ref, other_ref, previous_ref,
    through_ref, first_ref, second_ref, before_ref,
):
    core, x = place_ref[0], place_ref[1]
    width = mine_ref.shape[1]
    ahead = ahead_ref[...]
    start = start_factor_ref[width:] + product(ahead, start_factor_ref[:width])
    start = choose(x == 0, ahead, start)
    through_ref[0] = jnp.zeros(ahead.shape, F32)
    for i in range(1, own_ref.shape[0]):
        through_ref[i] = own_ref[i, width:] + product(ahead, own_ref[i, :width])
    both = functools.partial(both_cores, core, mine_ref, other_ref)
    factor_first, factor_second = both(0, width)
    inverse_first, inverse_second = both(2 * width, 3 * width)
    offset_first, offset_second = both(3 * width, mine_ref.shape[0])
    forward_first = offset_first + product(start, factor_first)
    forward_second = offset_second + product(forward_first, factor_second)
    first_ref[...] = product(forward_first, inverse_first)
    second_ref[...] = product(forward_second, inverse_second)
    previous = decode(previous_ref, (), width, slice(width, 2 * width))
    before_ref[...] = product(start, previous)


def backward_kernel(
    place_ref, size_ref, value_first, value_second, plane_first, plane_second,
    pair_first, pair_second, through_ref, mine_ref, other_ref, first_ref, second_ref, before_ref,
    previous_ref, leaf_forward_ref, far_upper_ref, far_upper_inv_ref, leaf_ref, sep_ref,
    leaf_upper_ref, leaf_upper_inv_ref, arrived,
):
    copies = [
        pltpu.make_async_copy(far_upper_ref, leaf_upper_ref, arrived.at[0]),
        pltpu.make_async_copy(far_upper_inv_ref, leaf_upper_inv_ref, arrived.at[1]),
    ]
    for copy in copies:
        copy.start()
    core, x, z = place_ref[0], place_ref[1], place_ref[2]
    planes, pairs = Wires(core, plane_first, plane_second), Wires(core, pair_first, pair_second)
    width = pairs.width
    backward = pair_columns(width)[1]
    received = jnp.zeros(first_ref.shape, F32)
    for i in range(planes.count - 1, 0, -1):
        mine, other = value_first[i].astype(F32), value_second[i].astype(F32)
        offset = [choose(core == 0, mine, other), choose(core == 0, other, mine)]
        further = jnp.concatenate(offset, axis=1)
        if i < planes.count - 1:
            further = further + product(received, planes.matrix(i))
        received = choose(z < i, further, received)
    chip = received
    for i in range(pairs.count - 1, 0, -1):
        received = through_ref[i] + product(received, pairs.matrix(i, backward))
        chip = choose(x < i, received, chip)
    factor_first, factor_second = both_cores(core, mine_ref, other_ref, width, 2 * width)
    second = second_ref[...] + product(chip, factor_second)
    first = first_ref[...] + product(second, factor_first)
    previous = decode(previous_ref, (), width, slice(0, width))
    before = before_ref[...] + product(first, previous)
    sep = choose(core == 0, first, second).T
    before = choose(core == 0, before, first).T.astype(BF16)
    sep_ref[...] = sep
    sep = sep.astype(BF16)
    dot = functools.partial(jnp.dot, preferred_element_type=F32)
    rows = lax.broadcasted_iota(jnp.int32, sep.shape, 0)
    for copy in copies:
        copy.wait()
    for leaf in range(leaf_ref.shape[0]):
        back = leaf_forward_ref[leaf] - dot(leaf_upper_ref[leaf, 0], before)
        back = back - dot(leaf_upper_ref[leaf, 1], sep)
        result = dot(leaf_upper_inv_ref[leaf], back.astype(BF16))
        leaf_ref[leaf] = jnp.where(rows < size_ref[leaf], result, 0.0)


def to_all(block, axis, dtype=F16):
    size = lax.axis_size(axis)
    slots = jnp.broadcast_to(block.astype(dtype)[None], (size,) + block.shape)
    return lax.all_to_all(slots, axis, 0, 0, tiled=True)


def swap_cores(block):
    return lax.ppermute(block, C, [(0, 1), (1, 0)])


def in_order(core, block):
    other = swap_cores(block)
    return block.astype(F32), other.astype(F32)


def per_device(
    leaf_rhs,
    sep_rhs,
    leaf_size,
    leaf_lower_inv,
    leaf_lower,
    leaf_upper,
    leaf_upper_inv,
    sep_lower_inv,
    sep_lower,
    sep_upper_inv,
    sep_upper,
):
    panel = (Z, X, C)
    panels = lax.axis_size(panel)
    planes, chips = lax.axis_size(Z), lax.axis_size(X)
    z, x, core = lax.axis_index(Z), lax.axis_index(X), lax.axis_index(C)
    place = jnp.stack([core, x, z]).astype(jnp.int32)
    leaves, width, samples = leaf_rhs.shape

    blocks = [sep_lower_inv[0], sep_lower[0], sep_upper_inv[0], sep_upper[0]]
    blocks = jnp.concatenate(blocks, axis=1)
    (wire,) = kernel(
        encode_rows_kernel, [wire_shape(*blocks.shape)], blocks
    )
    wire = to_all(wire, Y).astype(F32)

    active_rows = (jnp.arange(width, dtype=jnp.int32)[None, :] < leaf_size[:, None]).astype(F32)[
        :, :, None
    ]
    leaf_rounded = (active_rows * leaf_rhs).astype(BF16)
    leaf_forward = active_rows * jnp.einsum(
        "lij,ljs->lis", leaf_lower_inv, leaf_rounded, preferred_element_type=F32
    )
    forward_rounded = leaf_forward.astype(BF16)
    left_terms = jnp.einsum(
        "lij,ljs->is", leaf_lower[:, 0], forward_rounded, preferred_element_type=F32
    )
    from_right = lax.ppermute(left_terms, panel, [(i + 1, i) for i in range(panels - 1)])
    own_terms = jnp.einsum(
        "lij,ljs->is", leaf_lower[:, 1], forward_rounded, preferred_element_type=F32
    )

    mine, previous = kernel(
        factors_kernel,
        [shape(3 * width + samples, width), wire_shape(width, 2 * width)],
        wire,
        sep_rhs[0],
        own_terms,
        from_right,
    )
    other = swap_cores(mine)
    to_next_chip = [(i, i + 1) for i in range(1, panels - 1, 2)]
    previous = lax.ppermute(previous.astype(F16), panel, to_next_chip)
    part = width // 2
    (wire,) = kernel(pair_kernel, [wire_shape(part, 4 * width)], place, mine, other)

    pairs = in_order(core, to_all(wire, X))
    (wire,) = kernel(plane_kernel, [wire_shape(2, part, width + part)], place, *pairs)

    start, own = kernel(
        through_kernel,
        [shape(width + samples, width), shape(chips, width + samples, width)],
        place,
        *pairs,
    )
    wire, previous, start, own = lax.optimization_barrier(
        (wire.astype(F16), previous, start, own)
    )
    previous = previous.astype(F32)
    index = jnp.arange(planes, dtype=jnp.int32)[:, None, None]
    slots = jnp.where(index > z, wire[0][None], wire[1][None])
    between = in_order(core, lax.all_to_all(slots, Z, 0, 0, tiled=True))
    block = shape(samples, width)
    through = kernel(
        compose_kernel, [shape(width, part), shape(samples, part)], place, *pairs, own
    )
    wire, ahead = kernel(
        forward_kernel, [shape(samples, part, dtype=BF16), block], place, *between, *through
    )
    values = to_all(wire, Z, BF16)
    values = values, swap_cores(values)
    through, first, second, before = kernel(
        values_kernel,
        [shape(chips, samples, width), block, block, block],
        place,
        ahead,
        start,
        own,
        mine,
        other,
        previous,
    )

    leaf_correction, sep_correction = kernel(
        backward_kernel,
        [shape(leaves, width, samples), shape(width, samples)],
        place,
        leaf_size,
        *values,
        *between,
        *pairs,
        through,
        mine,
        other,
        first,
        second,
        before,
        previous,
        leaf_forward,
        left_in_hbm=[leaf_upper, leaf_upper_inv],
        scratch=[
            pltpu.VMEM(leaf_upper.shape, BF16),
            pltpu.VMEM(leaf_upper_inv.shape, BF16),
            pltpu.SemaphoreType.DMA((2,)),
        ],
    )
    return (leaf_correction, sep_correction[None])


def solution(mesh):
    cut = Mesh(mesh.devices.reshape(8, 4, 2, 8), (Z, X, C, Y))
    panel = (Z, X, C)
    return jax.shard_map(
        per_device,
        mesh=cut,
        in_specs=(
            P(panel, None, Y),
            P(panel, None, Y),
            P(panel),
            P(panel, None, None),
            P(panel, None, None, None),
            P(panel, None, None, None),
            P(panel, None, None),
            P(panel, Y, None),
            P(panel, Y, None),
            P(panel, Y, None),
            P(panel, Y, None),
        ),
        out_specs=(P(panel, None, Y), P(panel, None, Y)),
        check_vma=False,
    )
```

```python
import functools

import jax
import jax.numpy as jnp
from jax import lax
from jax.experimental import pallas as pl
from jax.experimental.pallas import tpu as pltpu
from jax.sharding import Mesh
from jax.sharding import PartitionSpec as P

Z, X, C, Y = "z", "x", "c", "y"
F32, F16, BF16 = jnp.float32, jnp.float16, jnp.bfloat16
LANES, EXTRA = 128, 8


def split(values):
    high = values.astype(BF16)
    return high, (values - high.astype(F32)).astype(BF16)


def product(left_side, right_side):
    left_high, left_low = split(left_side)
    right_high, right_low = split(right_side)
    rows = left_side.shape[0]
    dot = functools.partial(jnp.dot, preferred_element_type=F32)
    high = dot(jnp.concatenate([left_high, left_low], axis=0), right_high)
    return high[:rows] + (high[rows:] + dot(left_high, right_low))


def exponent(values, axis):
    largest = jnp.max(jnp.abs(values), axis=axis, keepdims=True)
    return jnp.clip(jnp.floor(jnp.log2(jnp.maximum(largest, 1e-36))), -120.0, 120.0)


def choose(condition, one, other):
    flags = jnp.zeros(one.shape, jnp.int32) + condition.astype(jnp.int32)
    return jnp.where(flags != 0, one, other)


def kernel(body, out_shapes, *operands, left_in_hbm=(), scratch=(), out=pltpu.VMEM, flops=0):
    moved = sum(o.size * o.dtype.itemsize for o in operands)
    moved += sum(o.size * o.dtype.itemsize for o in out_shapes)
    return pl.pallas_call(
        body,
        out_shape=out_shapes,
        in_specs=[
            pl.BlockSpec(memory_space=pltpu.SMEM if o.dtype == jnp.int32 else pltpu.VMEM)
            for o in operands
        ]
        + [pl.BlockSpec(memory_space=pltpu.HBM) for _ in left_in_hbm],
        out_specs=[pl.BlockSpec(memory_space=out) for _ in out_shapes],
        scratch_shapes=scratch,
        compiler_params=pltpu.CompilerParams(vmem_limit_bytes=16 * 2**20),
        cost_estimate=pl.CostEstimate(flops=flops, bytes_accessed=moved, transcendentals=0),
    )(*operands, *left_in_hbm)


def shape(*dims, dtype=F32):
    return jax.ShapeDtypeStruct(dims, dtype)


def half_rows(core, values):
    rows = values.shape[0] // 2
    return choose(core == 0, values[:rows], values[rows:])


def half_columns(core, values):
    columns = values.shape[1] // 2
    return choose(core == 0, values[:, :columns], values[:, columns:])


def wire_shape(*dims):
    *outer, rows, columns = dims
    return shape(*outer, columns // LANES * rows + EXTRA, LANES)


def encode(wire_ref, index, values):
    rows, columns = values.shape
    k = exponent(values, 0)
    scaled = values * jnp.exp2(-k)
    count = columns // LANES
    wire_ref[index + (slice(count * rows, None),)] = jnp.zeros((EXTRA, LANES), F32)
    for b in range(count):
        block = slice(LANES * b, LANES * (b + 1))
        wire_ref[index + (slice(rows * b, rows * (b + 1)),)] = scaled[:, block]
        wire_ref[index + (slice(count * rows + b, count * rows + b + 1),)] = k[:, block]


def decode(ref, index, rows, columns):
    count = (ref.shape[-2] - EXTRA) // rows
    blocks = []
    for b in range(columns.start // LANES, columns.stop // LANES):
        k = ref[index + (slice(count * rows + b, count * rows + b + 1),)]
        blocks.append(ref[index + (slice(rows * b, rows * (b + 1)),)] * jnp.exp2(k))
    return jnp.concatenate(blocks, axis=1)


class Wires:
    def __init__(self, core, mine_ref, other_ref):
        self.core, self.refs = core, (mine_ref, other_ref)
        self.count, self.part = mine_ref.shape[0], mine_ref.shape[2]
        self.width = 2 * self.part

    def in_order(self, i, columns):
        mine, other = (decode(ref, (i,), self.part, columns) for ref in self.refs)
        return [choose(self.core == 0, mine, other), choose(self.core == 0, other, mine)]

    def matrix(self, i, columns=None):
        columns = slice(0, self.width) if columns is None else columns
        return jnp.concatenate(self.in_order(i, columns), axis=0)

    def values(self, i, columns):
        return jnp.concatenate(self.in_order(i, columns), axis=1)

    def own_part(self, i, columns):
        return decode(self.refs[0], (i,), self.part, columns)


def pair_columns(width):
    part = width // 2
    starts = [0, width, 2 * width, 3 * width, 3 * width + part, 3 * width + 2 * part]
    return [slice(a, b) for a, b in zip(starts[:-1], starts[1:])]


def encode_rows_kernel(blocks_ref, wire_ref):
    encode(wire_ref, (), blocks_ref[...])


def factors_kernel(wire_ref, rhs_ref, own_ref, right_ref, out_ref, next_ref):
    width = rhs_ref.shape[0]
    senders = wire_ref.shape[0]

    def block(i):
        columns = slice(width * i, width * (i + 1))
        rows = [decode(wire_ref, (j,), width // senders, columns) for j in range(senders)]
        return jnp.concatenate(rows, axis=0).T

    source = (rhs_ref[...] - own_ref[...] - right_ref[...]).T
    both = product(jnp.concatenate([-block(1), source], axis=0), block(0))
    upper_inverse = block(2)
    out_ref[0:width] = both[:width]
    backward = product(-block(3), upper_inverse)
    out_ref[width : 2 * width] = backward
    out_ref[2 * width : 3 * width] = upper_inverse
    encode(next_ref, (), jnp.concatenate([backward, upper_inverse], axis=1))
    out_ref[3 * width :] = both[width:]


def both_cores(core, mine_ref, other_ref, start, end):
    mine, other = mine_ref[start:end], other_ref[start:end]
    return choose(core == 0, mine, other), choose(core == 0, other, mine)


def pair_kernel(place_ref, mine_ref, other_ref, wire_ref):
    core = place_ref[0]
    width = mine_ref.shape[1]
    both = functools.partial(both_cores, core, mine_ref, other_ref)
    forward_first, forward_second = both(0, width)
    backward_first, backward_second = both(width, 2 * width)
    inverse_first, inverse_second = both(2 * width, 3 * width)
    offset_first, offset_second = both(3 * width, mine_ref.shape[0])
    part = width // 2
    start = jnp.concatenate([half_rows(core, forward_first), offset_first], axis=0)
    end = product(start, forward_second)
    forward, value = end[:part], end[part:] + offset_second
    back = product(jnp.concatenate([forward, value], axis=0), inverse_second)
    back = jnp.concatenate([back, half_rows(core, backward_second)], axis=0)
    back = product(back, backward_first)
    rows = start.shape[0]
    through = product(start, inverse_first) + back[:rows]
    whole = [
        forward,
        back[rows:],
        through[:part],
        half_columns(core, value),
        half_columns(core, through[part:]),
    ]
    encode(wire_ref, (), jnp.concatenate(whole, axis=1))


def plane_kernel(place_ref, first_ref, second_ref, wire_ref):
    core = place_ref[0]
    pairs = Wires(core, first_ref, second_ref)
    part = pairs.width // 2
    forward, backward, _, value, _ = pair_columns(pairs.width)
    last = pairs.count - 1
    ahead = pairs.own_part(0, forward)
    ahead = jnp.concatenate([ahead, pairs.values(0, value)], axis=0)
    behind = pairs.own_part(last, backward)
    for i in range(1, pairs.count):
        ahead = product(ahead, pairs.matrix(i, forward))
        further = ahead[part:] + pairs.values(i, value)
        ahead = jnp.concatenate([ahead[:part], further], axis=0)
        behind = product(behind, pairs.matrix(last - i, backward))
    further = half_columns(core, ahead[part:])
    encode(wire_ref, (0,), jnp.concatenate([ahead[:part], further], axis=1))
    encode(wire_ref, (1,), jnp.concatenate([behind, further], axis=1))


def through_kernel(place_ref, mine_ref, other_ref, start_ref, own_ref):
    x = place_ref[1]
    pairs = Wires(place_ref[0], mine_ref, other_ref)
    width = pairs.width
    forward, _, through, value, back_value = pair_columns(width)

    def add_value(block, further):
        return jnp.concatenate([block[:width], block[width:] + further], axis=0)

    ahead = jnp.concatenate([pairs.matrix(0, forward), pairs.values(0, value)], axis=0)
    own = [jnp.concatenate([pairs.matrix(0, through), pairs.values(0, back_value)], axis=0)]
    start = ahead
    for i in range(1, pairs.count):
        start = choose(x == i, ahead, start)
        further = product(ahead, pairs.matrix(i, through))
        own.append(add_value(further, pairs.values(i, back_value)))
        if i < pairs.count - 1:
            further = product(ahead, pairs.matrix(i, forward))
            ahead = add_value(further, pairs.values(i, value))
    start_ref[...] = start
    for i in range(pairs.count):
        own_ref[i] = own[i]


def compose_kernel(place_ref, mine_ref, other_ref, own_ref, factor_ref, value_ref):
    pairs = Wires(place_ref[0], mine_ref, other_ref)
    width = pairs.width
    backward = pair_columns(width)[1]
    behind = own_ref[pairs.count - 1]
    for i in range(pairs.count - 2, -1, -1):
        factor, offset = pairs.matrix(i, backward), own_ref[i]
        if i == 0:
            factor, offset = half_columns(pairs.core, factor), half_columns(pairs.core, offset)
        behind = offset + product(behind, factor)
    factor_ref[...] = behind[:width]
    value_ref[...] = behind[width:]


def forward_kernel(
    place_ref, plane_mine, plane_other, factor_ref, value_ref, wire_ref, ahead_ref
):
    core, z = place_ref[0], place_ref[2]
    planes = Wires(core, plane_mine, plane_other)
    width = planes.width
    received = jnp.zeros(ahead_ref.shape, F32)
    for i in range(planes.count - 1):
        further = planes.values(i, slice(width, width + planes.part))
        if i > 0:
            further = further + product(received, planes.matrix(i))
        received = choose(z > i, further, received)
    ahead_ref[...] = received
    behind = value_ref[...] + product(received, factor_ref[...])
    wire_ref[...] = behind.astype(BF16)


def values_kernel(
    place_ref, ahead_ref, start_factor_ref, own_ref, mine_ref, other_ref, previous_ref,
    through_ref, first_ref, second_ref, before_ref,
):
    core, x = place_ref[0], place_ref[1]
    width = mine_ref.shape[1]
    ahead = ahead_ref[...]
    start = start_factor_ref[width:] + product(ahead, start_factor_ref[:width])
    start = choose(x == 0, ahead, start)
    through_ref[0] = jnp.zeros(ahead.shape, F32)
    for i in range(1, own_ref.shape[0]):
        through_ref[i] = own_ref[i, width:] + product(ahead, own_ref[i, :width])
    both = functools.partial(both_cores, core, mine_ref, other_ref)
    factor_first, factor_second = both(0, width)
    inverse_first, inverse_second = both(2 * width, 3 * width)
    offset_first, offset_second = both(3 * width, mine_ref.shape[0])
    forward_first = offset_first + product(start, factor_first)
    forward_second = offset_second + product(forward_first, factor_second)
    first_ref[...] = product(forward_first, inverse_first)
    second_ref[...] = product(forward_second, inverse_second)
    previous = decode(previous_ref, (), width, slice(width, 2 * width))
    before_ref[...] = product(start, previous)


def backward_kernel(
    place_ref, size_ref, value_first, value_second, plane_first, plane_second,
    pair_first, pair_second, through_ref, mine_ref, other_ref, first_ref, second_ref, before_ref,
    previous_ref, leaf_forward_ref, far_upper_ref, far_upper_inv_ref, far_leaf_ref, far_sep_ref,
    leaf_upper_ref, leaf_upper_inv_ref, leaf_ref, sep_ref, arrived, left,
):
    copies = [
        pltpu.make_async_copy(far_upper_ref, leaf_upper_ref, arrived.at[0]),
        pltpu.make_async_copy(far_upper_inv_ref, leaf_upper_inv_ref, arrived.at[1]),
    ]
    for copy in copies:
        copy.start()
    core, x, z = place_ref[0], place_ref[1], place_ref[2]
    planes, pairs = Wires(core, plane_first, plane_second), Wires(core, pair_first, pair_second)
    width = pairs.width
    backward = pair_columns(width)[1]
    received = jnp.zeros(first_ref.shape, F32)
    for i in range(planes.count - 1, 0, -1):
        mine, other = value_first[i].astype(F32), value_second[i].astype(F32)
        offset = [choose(core == 0, mine, other), choose(core == 0, other, mine)]
        further = jnp.concatenate(offset, axis=1)
        if i < planes.count - 1:
            further = further + product(received, planes.matrix(i))
        received = choose(z < i, further, received)
    chip = received
    for i in range(pairs.count - 1, 0, -1):
        received = through_ref[i] + product(received, pairs.matrix(i, backward))
        chip = choose(x < i, received, chip)
    factor_first, factor_second = both_cores(core, mine_ref, other_ref, width, 2 * width)
    second = second_ref[...] + product(chip, factor_second)
    first = first_ref[...] + product(second, factor_first)
    previous = decode(previous_ref, (), width, slice(0, width))
    before = before_ref[...] + product(first, previous)
    sep = choose(core == 0, first, second).T
    before = choose(core == 0, before, first).T.astype(BF16)
    sep_ref[...] = sep
    results = [pltpu.make_async_copy(sep_ref, far_sep_ref, left.at[0])]
    results[0].start()
    sep = sep.astype(BF16)
    dot = functools.partial(jnp.dot, preferred_element_type=F32)
    rows = lax.broadcasted_iota(jnp.int32, sep.shape, 0)
    for copy in copies:
        copy.wait()
    for leaf in range(leaf_ref.shape[0]):
        back = leaf_forward_ref[leaf] - dot(leaf_upper_ref[leaf, 0], before)
        back = back - dot(leaf_upper_ref[leaf, 1], sep)
        result = dot(leaf_upper_inv_ref[leaf], back.astype(BF16))
        leaf_ref[leaf] = jnp.where(rows < size_ref[leaf], result, 0.0)
        copy = pltpu.make_async_copy(leaf_ref.at[leaf], far_leaf_ref.at[leaf], left.at[leaf + 1])
        copy.start()
        results.append(copy)
    for copy in results:
        copy.wait()


def to_all(block, axis, dtype=F16):
    size = lax.axis_size(axis)
    slots = jnp.broadcast_to(block.astype(dtype)[None], (size,) + block.shape)
    return lax.all_to_all(slots, axis, 0, 0, tiled=True)


def swap_cores(block):
    return lax.ppermute(block, C, [(0, 1), (1, 0)])


def in_order(core, block):
    other = swap_cores(block)
    return block.astype(F32), other.astype(F32)


def per_device(
    leaf_rhs,
    sep_rhs,
    leaf_size,
    leaf_lower_inv,
    leaf_lower,
    leaf_upper,
    leaf_upper_inv,
    sep_lower_inv,
    sep_lower,
    sep_upper_inv,
    sep_upper,
):
    panel = (Z, X, C)
    panels = lax.axis_size(panel)
    planes, chips = lax.axis_size(Z), lax.axis_size(X)
    z, x, core = lax.axis_index(Z), lax.axis_index(X), lax.axis_index(C)
    place = jnp.stack([core, x, z]).astype(jnp.int32)
    leaves, width, samples = leaf_rhs.shape

    blocks = [sep_lower_inv[0], sep_lower[0], sep_upper_inv[0], sep_upper[0]]
    blocks = jnp.concatenate(blocks, axis=1)
    (wire,) = kernel(
        encode_rows_kernel, [wire_shape(*blocks.shape)], blocks
    )
    wire = to_all(wire, Y).astype(F32)

    active_rows = (jnp.arange(width, dtype=jnp.int32)[None, :] < leaf_size[:, None]).astype(F32)[
        :, :, None
    ]
    leaf_rounded = (active_rows * leaf_rhs).astype(BF16)
    leaf_forward = active_rows * jnp.einsum(
        "lij,ljs->lis", leaf_lower_inv, leaf_rounded, preferred_element_type=F32
    )
    forward_rounded = leaf_forward.astype(BF16)
    left_terms = jnp.einsum(
        "lij,ljs->is", leaf_lower[:, 0], forward_rounded, preferred_element_type=F32
    )
    from_right = lax.ppermute(left_terms, panel, [(i + 1, i) for i in range(panels - 1)])
    own_terms = jnp.einsum(
        "lij,ljs->is", leaf_lower[:, 1], forward_rounded, preferred_element_type=F32
    )

    mine, previous = kernel(
        factors_kernel,
        [shape(3 * width + samples, width), wire_shape(width, 2 * width)],
        wire,
        sep_rhs[0],
        own_terms,
        from_right,
    )
    other = swap_cores(mine)
    to_next_chip = [(i, i + 1) for i in range(1, panels - 1, 2)]
    previous = lax.ppermute(previous.astype(F16), panel, to_next_chip)
    part = width // 2
    (wire,) = kernel(pair_kernel, [wire_shape(part, 4 * width)], place, mine, other)

    pairs = in_order(core, to_all(wire, X))
    (wire,) = kernel(plane_kernel, [wire_shape(2, part, width + part)], place, *pairs)

    start, own = kernel(
        through_kernel,
        [shape(width + samples, width), shape(chips, width + samples, width)],
        place,
        *pairs,
    )
    wire, previous, start, own = lax.optimization_barrier(
        (wire.astype(F16), previous, start, own)
    )
    previous = previous.astype(F32)
    index = jnp.arange(planes, dtype=jnp.int32)[:, None, None]
    slots = jnp.where(index > z, wire[0][None], wire[1][None])
    between = in_order(core, lax.all_to_all(slots, Z, 0, 0, tiled=True))
    block = shape(samples, width)
    through = kernel(
        compose_kernel, [shape(width, part), shape(samples, part)], place, *pairs, own
    )
    wire, ahead = kernel(
        forward_kernel, [shape(samples, part, dtype=BF16), block], place, *between, *through
    )
    values = to_all(wire, Z, BF16)
    values = values, swap_cores(values)
    through, first, second, before = kernel(
        values_kernel,
        [shape(chips, samples, width), block, block, block],
        place,
        ahead,
        start,
        own,
        mine,
        other,
        previous,
    )

    leaf_correction, sep_correction = kernel(
        backward_kernel,
        [shape(leaves, width, samples), shape(width, samples)],
        place,
        leaf_size,
        *values,
        *between,
        *pairs,
        through,
        mine,
        other,
        first,
        second,
        before,
        previous,
        leaf_forward,
        left_in_hbm=[leaf_upper, leaf_upper_inv],
        scratch=[
            pltpu.VMEM(leaf_upper.shape, BF16),
            pltpu.VMEM(leaf_upper_inv.shape, BF16),
            pltpu.VMEM((leaves, width, samples), F32),
            pltpu.VMEM((width, samples), F32),
            pltpu.SemaphoreType.DMA((2,)),
            pltpu.SemaphoreType.DMA((leaves + 1,)),
        ],
        out=pltpu.HBM,
    )
    return (leaf_correction, sep_correction[None])


def solution(mesh):
    cut = Mesh(mesh.devices.reshape(8, 4, 2, 8), (Z, X, C, Y))
    panel = (Z, X, C)
    return jax.shard_map(
        per_device,
        mesh=cut,
        in_specs=(
            P(panel, None, Y),
            P(panel, None, Y),
            P(panel),
            P(panel, None, None),
            P(panel, None, None, None),
            P(panel, None, None, None),
            P(panel, None, None),
            P(panel, Y, None),
            P(panel, Y, None),
            P(panel, Y, None),
            P(panel, Y, None),
        ),
        out_specs=(P(panel, None, Y), P(panel, None, Y)),
        check_vma=False,
    )
```
